256 devices in a mesh: ctx: 16 (over y, x), exp: 16 (over z, core).
Axes of the slice: x: 4, y: 4, z: 8, core: 2. Of those that a mesh axis runs over, the one named last changes fastest.
Arguments:
- queries: bfloat16 [16, 2048, 4096], P('exp', 'ctx'), may hold values from -0.29882812 to 0.29882812
- keys: bfloat16 [16, 2048, 4096], P('exp', 'ctx'), may hold values from -0.29882812 to 0.29882812
- values: bfloat16 [16, 2048, 4096], P('exp', 'ctx'), may hold values from -0.29882812 to 0.29882812
- out_grad: bfloat16 [16, 2048, 4096], P('exp', 'ctx'), may hold values from -6 to 6
- log_decay: float32 [16, 32, 2048], P('exp', None, 'ctx'), may hold values from -1 to 0
- doc_lengths: int32 [16, 4], P('exp'), may hold values from 1 to 1025, 2048 in all within a row
- moe_input: bfloat16 [2048, 3072], P(('ctx', 'exp')), may hold values from -6 to 6
- moe_grad: bfloat16 [2048, 3072], P(('ctx', 'exp')), may hold values from -6 to 6
- routes: int32 [2048, 2], P(('ctx', 'exp')), may hold values from 0 to 15, all different within a row; in each aligned block of 8 rows (0 to 7, 8 to 15, ...) at most 2 rows name the same one
- gate_weights: float32 [2048, 2], P(('ctx', 'exp')), may hold values from 0.1 to 0.9
- w_gate: bfloat16 [16, 4608, 3072], P('exp', 'ctx'), may hold values from -0.109375 to 0.109375
- w_up: bfloat16 [16, 4608, 3072], P('exp', 'ctx'), may hold values from -0.109375 to 0.109375
- w_down: bfloat16 [16, 4608, 3072], P('exp', 'ctx'), may hold values from -0.09375 to 0.09375
Outputs:
- d_queries: bfloat16 [16, 2048, 4096], P('exp', 'ctx')
- d_keys: bfloat16 [16, 2048, 4096], P('exp', 'ctx')
- d_values: bfloat16 [16, 2048, 4096], P('exp', 'ctx')
- d_moe_input: bfloat16 [2048, 3072], P(('ctx', 'exp'))
The draws below stay inside these ranges and needn't reach their ends.
Inputs may be any that keep to these rules, and one draw needn't show every extreme that they name: `doc_lengths`: each row sums to 2048 and its longest document has 1025 positions. `routes`: two different experts a row; among the 8 rows of one device no expert is named more than 2 times.
All inputs are finite; a program needn't handle non-finite values.
Results may differ from the reference program's by a relative error of at most 0.02.
Values may be sent and summed in bfloat16 or wider, within the bound.
No kernel may reach another device: no remote copies, remote signals or barrier semaphores. Data moves between devices by JAX's collectives and lax.ppermute only.
A program may use at most 192 MiB of HBM per device.

```python
import math
from functools import partial
import jax
import jax.numpy as jnp
import numpy as np
from jax import lax

ATTN_COUNT = 32
DH = 128
D = 3072
FF = 4608
TOP = 2
DOCS = 4
TOK_DEV = 128
MOE_TOK = 8
CONTEXT_LENGTH = 2048
HD = 4096
EXPERTS = 16
CAP = 2
MOE_TOKENS = 2048
N_CTX = 16
N_EXP = 16


def draw_log_decay(key, part):
    key = jax.random.fold_in(key, 7)
    draw_keys = jax.random.split(key, 8)
    slow_share = 0.5
    shape_heads = (N_EXP, ATTN_COUNT, 1)
    shape_full = (N_EXP, ATTN_COUNT, CONTEXT_LENGTH)
    slow_heads = jax.random.uniform(draw_keys[0], shape_heads) < slow_share
    slow_rate = jax.random.uniform(draw_keys[1], shape_heads, minval=0.25, maxval=0.75) / CONTEXT_LENGTH
    fast_rate = jax.random.uniform(draw_keys[2], shape_heads, minval=2.0 / 50.0, maxval=2.0 / 30.0)
    block_modes = jax.random.randint(draw_keys[6], (N_EXP, ATTN_COUNT, N_CTX), 0, 3)
    mode_steps = jnp.repeat(block_modes, TOK_DEV, axis=2)
    places = jnp.arange(CONTEXT_LENGTH, dtype=jnp.int32) % TOK_DEV
    rim_places = (places < 3) | (places >= TOK_DEV - 3)
    fast_block = jnp.logical_not(slow_heads) & (mode_steps == 1)
    rim_block = jnp.logical_not(slow_heads) & (mode_steps == 2) & rim_places[None, None, :]
    nominal_speed = jnp.where(fast_block, fast_rate, slow_rate)
    random_offset = jnp.exp(jax.random.uniform(draw_keys[3], shape_full, minval=-0.7, maxval=0.7))
    sudden_spikes = jax.random.uniform(draw_keys[4], shape_full) < 2.0 / CONTEXT_LENGTH
    spike_depth = jnp.log(jax.random.uniform(draw_keys[5], shape_full, minval=0.5, maxval=0.8))
    rim_depth = jax.random.uniform(draw_keys[7], shape_full, minval=-0.9, maxval=-0.8)
    extra_fade = jnp.where(rim_block, rim_depth, jnp.where(sudden_spikes, spike_depth, 0.0))
    natural_log_fades = -nominal_speed * random_offset + extra_fade
    return natural_log_fades.astype(jnp.float32)


def level_of(stream_key, shape, shards, low, top_value):
    def one(position, shards_of):
        heights = jax.random.uniform(jax.random.fold_in(jax.random.fold_in(stream_key, 6), position), (shards_of,), jnp.float32, low / len(shards), top_value / len(shards))
        return jnp.repeat(jnp.exp(heights), shape[position] // shards_of).reshape((-1,) + (1,) * (len(shape) - position - 1))

    factor_of = one(*shards[0])
    for cut in shards[1:]:
        factor_of = factor_of * one(*cut)
    return factor_of


def split_up(amount, total, bound, lean):
    portions = [(1 << 20) // math.isqrt(standing ** lean) + 1 for standing in range(2, amount + 1)]
    spare, given = total - bound - (amount - 1), [1] * (amount - 1)
    while spare > 0:
        free = [i for i in range(amount - 1) if given[i] < bound]
        pool, remaining = sum([portions[i] for i in free]), spare
        for i in free:
            more = min(bound - given[i], max(1, remaining * portions[i] // pool), spare)
            given[i] = given[i] + more
            spare = spare - more
    return np.array([bound] + given)


def uneven_parts(rng, count, total, limit, slope):
    if count == 2:
        one = jax.random.randint(rng, (), max(1, total - limit), min(limit, total - 1) + 1)
        return jnp.stack([one, total - one])
    sizes = jnp.asarray(split_up(count, total, limit, slope), jnp.int32)
    pairs = (count - 1) // 2
    source_of, taker = sizes[1:1 + 2 * pairs:2], sizes[2:2 + 2 * pairs:2]
    margin = jnp.minimum(source_of - 1, limit - taker)
    moved = jax.random.randint(jax.random.fold_in(rng, 1), (pairs,), 0, 1 << 20) % (margin + 1)
    sizes = sizes.at[1:1 + 2 * pairs:2].set(source_of - moved).at[2:2 + 2 * pairs:2].set(taker + moved)
    return sizes[jax.random.permutation(jax.random.fold_in(rng, 2), count)]


def shared_out(stream_key, own, number, rows, count, top, most, lean):
    sequence = jax.random.permutation(stream_key, count)
    packed, usual = load_shares(count, rows * top, most, lean, True), load_shares(count, rows * top, most, lean, False)
    places = jnp.arange(count)

    def named(tallies, turn):
        used = int((tallies > 0).sum())
        fixed = max(1, used // 4)
        shifted = fixed + (places - fixed + turn * (used - fixed)) % max(1, count - fixed)
        return jnp.zeros((count,), jnp.int32).at[sequence[jnp.where(places < fixed, places, shifted)]].set(jnp.asarray(tallies, jnp.int32))

    tallies = jnp.where(number % 4 == 0, named(packed, number // 4), named(usual, number - number // 4 - 1))
    mixed = jax.random.permutation(jax.random.fold_in(own, 3), count)
    giver, sink = mixed[0:count // 2 * 2:2], mixed[1:count // 2 * 2:2]
    slack = jnp.minimum(tallies[giver] - 1, most - tallies[sink]) // 2
    slack = jnp.where((giver == sequence[0]) | (sink == sequence[0]) | (tallies[sink] == 0), 0, jnp.maximum(slack, 0))
    shifted = jax.random.randint(jax.random.fold_in(own, 4), (count // 2,), 0, 1 << 20) % (slack + 1)
    tallies = tallies.at[giver].add(-shifted).at[sink].add(shifted)
    labels = jnp.searchsorted(jnp.cumsum(tallies), jnp.arange(rows * top), side="right").astype(jnp.int32)
    grid = labels.reshape(top, rows).T
    grid = grid[jax.random.permutation(jax.random.fold_in(own, 1), rows)]
    turn = jax.random.randint(jax.random.fold_in(own, 2), (rows, 1), 0, top)
    return jnp.take_along_axis(grid, (jnp.arange(top)[None, :] + turn) % top, axis=1)


def load_shares(count, total, limit, slope, full):
    portions = [(1 << 20) // math.isqrt(standing ** slope) + 1 for standing in range(1, count + 1)]
    largest = limit if full else min(limit, max(-(-total // count), total * portions[0] // sum(portions)))
    least = 1 if total - largest >= count - 1 else 0
    counts, surplus = [largest] + [least] * (count - 1), total - largest - least * (count - 1)
    while surplus > 0:
        free = [i for i in range(1, count) if counts[i] < largest] or [i for i in range(1, count) if counts[i] < limit]
        pool, budget = sum([portions[i] for i in free]), surplus
        for i in free:
            extra = min(limit - counts[i], max(1, budget * portions[i] // pool), surplus)
            counts[i] = counts[i] + extra
            surplus = surplus - extra
    return np.array(counts)


def scatter_about(stream_key, shape, scale, limit, pieces=(), held_as=jnp.bfloat16):
    entries = jax.random.normal(stream_key, shape, jnp.float32) * scale
    if len(pieces) > 0:
        entries = level_of(stream_key, shape, pieces, -0.22, 0.18) * entries
    return jnp.clip(entries, min=-limit, max=limit).astype(held_as)


def setup_inputs(seed: int = 0) -> dict:
    key_of = jax.random.split(jax.random.key(seed), 14)
    queries = scatter_about(key_of[0], (N_EXP, CONTEXT_LENGTH, HD), 0.05, 0.29882812, ((0, 16), (1, 16)))
    keys = scatter_about(key_of[1], (N_EXP, CONTEXT_LENGTH, HD), 0.05, 0.29882812, ((0, 16), (1, 16)))
    values = scatter_about(key_of[2], (N_EXP, CONTEXT_LENGTH, HD), 0.05, 0.29882812, ((0, 16), (1, 16)))
    out_grad = scatter_about(key_of[3], (N_EXP, CONTEXT_LENGTH, HD), 1.0, 6.0, ((0, 16), (1, 16)))
    log_decay = draw_log_decay(jax.random.fold_in(key_of[13], 71), 0)
    doc_lengths = jax.vmap(lambda own: uneven_parts(own, DOCS, CONTEXT_LENGTH, CONTEXT_LENGTH // 2 + 1, 2))(jax.random.split(key_of[5], N_EXP)).reshape((N_EXP, DOCS)).astype(jnp.int32)
    moe_input = scatter_about(key_of[6], (MOE_TOKENS, D), 1.0, 6.0, ((0, 256),))
    moe_grad = scatter_about(key_of[7], (MOE_TOKENS, D), 1.0, 6.0, ((0, 256),))
    routes_keys = jax.random.split(jax.random.fold_in(key_of[8], 1), MOE_TOKENS // MOE_TOK)
    routes_turns = jax.random.permutation(jax.random.fold_in(key_of[8], 3), MOE_TOKENS // MOE_TOK)
    routes = jax.vmap(lambda own, number: shared_out(jax.random.fold_in(key_of[8], 2), own, number, MOE_TOK, EXPERTS, TOP, CAP, 2))(routes_keys, routes_turns).reshape((MOE_TOKENS, TOP))
    gate_weights = jnp.clip(0.1 + 0.79999997 * jax.random.uniform(key_of[9], (MOE_TOKENS, TOP), jnp.float32) ** level_of(key_of[9], (MOE_TOKENS, TOP), ((0, 256),), -0.2, 0.2), 0.1, 0.9)
    w_gate = scatter_about(key_of[10], (EXPERTS, FF, D), D ** -0.5, 0.109375, ((0, 16), (1, 16)))
    w_up = scatter_about(key_of[11], (EXPERTS, FF, D), D ** -0.5, 0.109375, ((0, 16), (1, 16)))
    w_down = scatter_about(key_of[12], (EXPERTS, FF, D), FF ** -0.5, 0.09375, ((0, 16), (1, 16)))
    return {"queries": queries, "keys": keys, "values": values, "out_grad": out_grad, "log_decay": log_decay, "doc_lengths": doc_lengths, "moe_input": moe_input, "moe_grad": moe_grad, "routes": routes, "gate_weights": gate_weights, "w_gate": w_gate, "w_up": w_up, "w_down": w_down}


def product(form, left, right):
    return jnp.einsum(form, left.astype(jnp.float32), right.astype(jnp.float32))


def decay_tables(natural_log_fades, starts):
    segment = jnp.cumsum(starts.astype(jnp.int32))
    running = jnp.cumsum(natural_log_fades, axis=1)
    length = natural_log_fades.shape[1]
    places = jnp.arange(length, dtype=jnp.int32)
    linked = (segment[:, None] == segment[None, :]) & (places[:, None] >= places[None, :])
    spread = jnp.where(linked[None], running[:, :, None] - running[:, None, :], 0.0)
    within = jnp.where(linked[None], jnp.exp(spread), 0.0)
    from_start = jnp.exp(running) * (segment == 0)[None, :]
    to_end = jnp.exp(running[:, -1:] - running) * (segment == segment[-1])[None, :]
    return within, from_start, to_end, from_start[:, -1]


def local_sums(query_rows, key_rows, value_rows, grad_rows, from_start, to_end):
    keys_end = (key_rows.astype(jnp.float32) * to_end.T[:, :, None]).astype(jnp.bfloat16)
    queries_start = (query_rows.astype(jnp.float32) * from_start.T[:, :, None]).astype(jnp.bfloat16)
    state_local = product("shd,she->hde", keys_end, value_rows)
    grad_local = product("uhd,uhe->hde", queries_start, grad_rows)
    return state_local, grad_local


def block_grads(query_rows, key_rows, value_rows, grad_rows, within, from_start, to_end, state_in, carried):
    state_half = state_in.astype(jnp.bfloat16)
    carried_half = carried.astype(jnp.bfloat16)
    flipped = jnp.swapaxes(within, 1, 2)
    weight_q = (product("the,she->hts", grad_rows, value_rows) * within).astype(jnp.bfloat16)
    weight_k = (product("the,uhe->htu", value_rows, grad_rows) * flipped).astype(jnp.bfloat16)
    weight_v = (product("thd,uhd->htu", key_rows, query_rows) * flipped).astype(jnp.bfloat16)
    grad_q = product("hts,shd->thd", weight_q, key_rows) + from_start.T[:, :, None] * product("the,hde->thd", grad_rows, state_half)
    grad_k = product("htu,uhd->thd", weight_k, query_rows) + to_end.T[:, :, None] * product("the,hde->thd", value_rows, carried_half)
    grad_v = product("htu,uhe->the", weight_v, grad_rows) + to_end.T[:, :, None] * product("thd,hde->the", key_rows, carried_half)
    return grad_q.astype(jnp.bfloat16), grad_k.astype(jnp.bfloat16), grad_v.astype(jnp.bfloat16)


def attention_row(items):
    query_row, key_row, value_row, grad_row, rate_row, lengths_row = items

    def blocked(array):
        return array.reshape(N_CTX, TOK_DEV, ATTN_COUNT, DH)

    doc_starts = jnp.cumsum(lengths_row) - lengths_row
    positions = jnp.arange(CONTEXT_LENGTH, dtype=jnp.int32)
    starts = jnp.any(positions[:, None] == doc_starts[None, :], axis=1).reshape(N_CTX, TOK_DEV)
    natural_log_fades = rate_row.reshape(ATTN_COUNT, N_CTX, TOK_DEV).transpose(1, 0, 2)
    within, from_start, to_end, block_decay = jax.vmap(decay_tables)(natural_log_fades, starts)
    query_b, key_b, value_b, grad_b = blocked(query_row), blocked(key_row), blocked(value_row), blocked(grad_row)
    state_local, grad_local = jax.vmap(local_sums)(query_b, key_b, value_b, grad_b, from_start, to_end)
    empty = jnp.zeros((ATTN_COUNT, DH, DH), jnp.float32)

    def forward_step(carry, item):
        return item[0][:, None, None] * carry + item[1], carry

    def backward_step(carry, item):
        return item[1] + item[0][:, None, None] * carry, carry

    _, state_in = lax.scan(forward_step, empty, (block_decay, state_local))
    _, carried = lax.scan(backward_step, empty, (block_decay, grad_local), reverse=True)
    grads = jax.vmap(block_grads)(query_b, key_b, value_b, grad_b, within, from_start, to_end, state_in, carried)
    return tuple(piece.reshape(CONTEXT_LENGTH, ATTN_COUNT * DH) for piece in grads)


def slot_table(route_ids, capacity, experts):
    flat_ids = route_ids.reshape(-1)
    route_count = flat_ids.shape[0]
    onehot_ids = (flat_ids[:, None] == jnp.arange(experts, dtype=jnp.int32)[None, :]).astype(jnp.int32)
    earlier = jnp.cumsum(onehot_ids, axis=0) - onehot_ids
    ranks = jnp.sum(earlier * onehot_ids, axis=1)
    slots = flat_ids * capacity + ranks
    matches = slots[None, :] == jnp.arange(experts * capacity, dtype=jnp.int32)[:, None]
    filled = jnp.any(matches, axis=1)
    sources = jnp.sum(jnp.where(matches, jnp.arange(route_count, dtype=jnp.int32)[None, :], 0), axis=1)
    return slots, filled, sources


def fill_slots(token_rows, scaled_rows, route_ids, capacity, experts):
    slots, filled, sources = slot_table(route_ids, capacity, experts)
    input_slots = jnp.where(filled[:, None], token_rows[sources // 2], jnp.zeros((), token_rows.dtype))
    grad_slots = jnp.where(filled[:, None], scaled_rows[sources], jnp.zeros((), scaled_rows.dtype))
    width = token_rows.shape[1]
    return input_slots.reshape(experts, capacity, width), grad_slots.reshape(experts, capacity, width)


def scale_grads(grad_rows, gate_rows):
    doubled = jnp.repeat(grad_rows, 2, axis=0).astype(jnp.float32)
    return (gate_rows.reshape(-1)[:, None] * doubled).astype(jnp.bfloat16)


def expert_grads(input_rows, grad_rows, gate_slab, up_slab, down_slab):
    contract = (((1,), (1,)), ((), ()))
    gate_value = lax.dot_general(input_rows, gate_slab, contract, preferred_element_type=jnp.float32)
    up_value = lax.dot_general(input_rows, up_slab, contract, preferred_element_type=jnp.float32)
    hidden_grad = lax.dot_general(grad_rows, down_slab, contract, preferred_element_type=jnp.float32)
    sigmoid = jax.nn.sigmoid(gate_value)
    grad_up = (hidden_grad * gate_value * sigmoid).astype(jnp.bfloat16)
    grad_gate = (hidden_grad * up_value * sigmoid * (1.0 + gate_value * (1.0 - sigmoid))).astype(jnp.bfloat16)
    return jnp.dot(grad_gate, gate_slab, preferred_element_type=jnp.float32) + jnp.dot(grad_up, up_slab, preferred_element_type=jnp.float32)


def moe_grads(moe_input, moe_grad, routes, gate_weights, w_gate, w_up, w_down):
    dev_count = N_CTX * N_EXP
    inputs_dev = moe_input.reshape(dev_count, MOE_TOK, D)
    grads_dev = moe_grad.reshape(dev_count, MOE_TOK, D)
    routes_dev = routes.reshape(dev_count, MOE_TOK, TOP)
    gates_dev = gate_weights.reshape(dev_count, MOE_TOK, TOP)
    scaled = jax.vmap(scale_grads)(grads_dev, gates_dev)
    filler = partial(fill_slots, capacity=CAP, experts=EXPERTS)
    slot_in, slot_grad = jax.vmap(filler)(inputs_dev, scaled, routes_dev)
    expert_in = jnp.moveaxis(slot_in, 1, 0)
    expert_grad = jnp.moveaxis(slot_grad, 1, 0)
    slice_width = FF // N_CTX

    def one_expert(items):
        rows_in, rows_grad, gate_full, up_full, down_full = items
        flat_in = rows_in.reshape(-1, D)
        flat_grad = rows_grad.reshape(-1, D)
        slabs = (gate_full.reshape(N_CTX, slice_width, D), up_full.reshape(N_CTX, slice_width, D), down_full.reshape(N_CTX, slice_width, D))

        def slice_step(total, slab_set):
            term = expert_grads(flat_in, flat_grad, slab_set[0], slab_set[1], slab_set[2])
            rounded = lax.optimization_barrier(term.astype(jnp.bfloat16))
            return total + rounded.astype(jnp.float32), None

        total, _ = lax.scan(slice_step, jnp.zeros(flat_in.shape, jnp.float32), slabs)
        return total.astype(jnp.bfloat16).reshape(rows_in.shape)

    results = lax.map(one_expert, (expert_in, expert_grad, w_gate, w_up, w_down))
    per_dev = jnp.moveaxis(results, 0, 1).reshape(dev_count, EXPERTS * CAP, D)

    def combine_dev(rows, route_ids):
        slots = slot_table(route_ids, CAP, EXPERTS)[0]
        return rows[slots].astype(jnp.float32).reshape(MOE_TOK, TOP, D).sum(axis=1).astype(jnp.bfloat16)

    return jax.vmap(combine_dev)(per_dev, routes_dev).reshape(MOE_TOKENS, D)


def reference(queries, keys, values, out_grad, log_decay, doc_lengths, moe_input, moe_grad, routes, gate_weights, w_gate, w_up, w_down):
    d_queries, d_keys, d_values = lax.map(attention_row, (queries, keys, values, out_grad, log_decay, doc_lengths))
    d_moe_input = moe_grads(moe_input, moe_grad, routes, gate_weights, w_gate, w_up, w_down)
    return (d_queries, d_keys, d_values, d_moe_input)
```

```python
import functools

import jax
import jax.numpy as jnp
from jax import lax
from jax.experimental import pallas as pl
from jax.experimental.pallas import tpu as pltpu
from jax.sharding import PartitionSpec as P

F32 = jnp.float32
BF16 = jnp.bfloat16
NT = (((1,), (1,)), ((), ()))
TN = (((0,), (0,)), ((), ()))
HEADS_STEP = 8
DECAY_ROWS = 16


def dot(a, b, dims=(((1,), (0,)), ((), ()))):
    return lax.dot_general(a, b, dims, preferred_element_type=F32)


def exact_dot(a, b, dims=(((1,), (0,)), ((), ()))):
    return lax.dot_general(
        a, b, dims, precision=lax.Precision.HIGHEST, preferred_element_type=F32
    )


def segments(lengths_ref, place_ref, length, axis):
    shape = (length, 1) if axis == 0 else (1, length)
    base = place_ref[0] * length
    at = lax.broadcasted_iota(jnp.int32, shape, axis) + base
    count = jnp.zeros(shape, jnp.int32)
    start = jnp.int32(0)
    for doc in range(lengths_ref.shape[1]):
        inside = jnp.where(start >= base, 1, 0)
        count = count + jnp.where(at >= start, inside, 0)
        start = start + lengths_ref[0, doc]
    last = jnp.int32(0)
    start = jnp.int32(0)
    for doc in range(lengths_ref.shape[1]):
        last = last + jnp.where((start >= base) & (start < base + length), 1, 0)
        start = start + lengths_ref[0, doc]
    return count, last


def running_sums(log_ref, length):
    logs = log_ref[...]
    low = lax.broadcasted_iota(jnp.int32, (length, length), 0)
    high = lax.broadcasted_iota(jnp.int32, (length, length), 1)
    upper = jnp.where(low <= high, 1.0, 0.0).astype(F32)
    rows = exact_dot(logs, upper)
    return rows, rows.T


def local_kernel(lengths_ref, place_ref, log_ref, q_ref, k_ref, v_ref, g_ref, out_ref):
    length = q_ref.shape[0]
    size = q_ref.shape[1] // HEADS_STEP
    seg, last = segments(lengths_ref, place_ref, length, 0)
    rows, cols = running_sums(log_ref, length)
    first_doc = jnp.where(seg == 0, 1.0, 0.0).astype(F32)
    last_doc = jnp.where(seg == last, 1.0, 0.0).astype(F32)
    whole = jnp.where(last == 0, 1.0, 0.0).astype(F32)
    row_id = lax.broadcasted_iota(jnp.int32, (DECAY_ROWS, size), 0)
    for pair in range(HEADS_STEP // 2):
        pieces = jnp.zeros((DECAY_ROWS, size), F32)
        for own in range(2):
            head = 2 * pair + own
            at = slice(head * size, (head + 1) * size)
            col = cols[:, head : head + 1]
            end = cols[length - 1 : length, head : head + 1]
            from_start = jnp.exp(col) * first_doc
            to_end = jnp.exp(end - col) * last_doc
            keys_end = (k_ref[:, at].astype(F32) * to_end).astype(BF16)
            queries_start = (q_ref[:, at].astype(F32) * from_start).astype(BF16)
            out_ref[pair, own * size : (own + 1) * size, :] = dot(
                keys_end, v_ref[:, at], TN
            ).astype(BF16)
            out_ref[pair, (2 + own) * size : (3 + own) * size, :] = dot(
                queries_start, g_ref[:, at], TN
            ).astype(BF16)
            rest = jnp.broadcast_to(jnp.exp(end) * whole, (DECAY_ROWS, size))
            for part in range(3):
                piece = rest.astype(BF16).astype(F32)
                pieces = jnp.where(row_id == own * 8 + part, piece, pieces)
                rest = rest - piece
        out_ref[pair, 4 * size :, :] = pieces.astype(BF16)


def scan_kernel(in_ref, out_ref):
    blocks = in_ref.shape[0]
    size = in_ref.shape[2]

    def decay(block, own):
        rows = in_ref[block, 4 * size :, :].astype(F32)
        at = own * 8
        return rows[at : at + 1] + rows[at + 1 : at + 2] + rows[at + 2 : at + 3]

    for own in range(2):
        for kind in range(2):
            at = slice((2 * kind + own) * size, (2 * kind + own + 1) * size)
            carry = jnp.zeros((size, size), F32)
            order = range(blocks) if kind == 0 else range(blocks - 1, -1, -1)
            for block in order:
                out_ref[block, at, :] = carry.astype(BF16)
                carry = decay(block, own) * carry + in_ref[block, at, :].astype(F32)


def grads_kernel(
    lengths_ref, place_ref, log_ref, q_ref, k_ref, v_ref, g_ref, s_ref, dq_ref, dk_ref, dv_ref
):
    length = q_ref.shape[0]
    size = q_ref.shape[1] // HEADS_STEP
    seg, last = segments(lengths_ref, place_ref, length, 0)
    seg_row, _ = segments(lengths_ref, place_ref, length, 1)
    rows, cols = running_sums(log_ref, length)
    first_doc = jnp.where(seg == 0, 1.0, 0.0).astype(F32)
    last_doc = jnp.where(seg == last, 1.0, 0.0).astype(F32)
    low = lax.broadcasted_iota(jnp.int32, (length, length), 0)
    high = lax.broadcasted_iota(jnp.int32, (length, length), 1)
    linked = (low >= high) & (seg == seg_row)
    for head in range(HEADS_STEP):
        at = slice(head * size, (head + 1) * size)
        pair, own = head // 2, head % 2
        col = cols[:, head : head + 1]
        end = cols[length - 1 : length, head : head + 1]
        from_start = jnp.exp(col) * first_doc
        to_end = jnp.exp(end - col) * last_doc
        within = jnp.exp(jnp.where(linked, col - rows[head : head + 1, :], -1e9))
        q, k, v, g = q_ref[:, at], k_ref[:, at], v_ref[:, at], g_ref[:, at]
        state = s_ref[pair, own * size : (own + 1) * size, :]
        carried = s_ref[pair, (2 + own) * size : (3 + own) * size, :]
        weight_q = (dot(g, v, NT) * within).astype(BF16)
        weight_v = (dot(q, k, NT) * within).astype(BF16)
        dq_ref[:, at] = (dot(weight_q, k) + from_start * dot(g, state, NT)).astype(BF16)
        dk_ref[:, at] = (dot(weight_q, q, TN) + to_end * dot(v, carried, NT)).astype(BF16)
        dv_ref[:, at] = (dot(weight_v, g, TN) + to_end * dot(k, carried)).astype(BF16)


def slot_numbers(routes_ref):
    tokens, top = routes_ref.shape
    flat = [routes_ref[i, k] for i in range(tokens) for k in range(top)]
    slots = []
    for r, expert in enumerate(flat):
        rank = jnp.int32(0)
        for earlier in flat[:r]:
            rank = rank + jnp.where(earlier == expert, 1, 0)
        slots.append(2 * expert + rank)
    return slots


def fill_kernel(routes_ref, gates_ref, in_ref, grad_ref, out_ref):
    tokens, width = in_ref.shape
    top = routes_ref.shape[1]
    count = out_ref.shape[0]
    slots = slot_numbers(routes_ref)
    row = lax.broadcasted_iota(jnp.int32, (count, tokens), 0)
    col = lax.broadcasted_iota(jnp.int32, (count, tokens), 1)
    row_one = lax.broadcasted_iota(jnp.int32, (count, 1), 0)
    pick = jnp.zeros((count, tokens), F32)
    gate = jnp.zeros((count, 1), F32)
    for r, slot in enumerate(slots):
        pick = jnp.where((row == slot) & (col == r // top), 1.0, pick)
        gate = jnp.where(row_one == slot, gates_ref[r // top, r % top], gate)
    pick = pick.astype(BF16)
    out_ref[:, :width] = dot(pick, in_ref[...]).astype(BF16)
    out_ref[:, width:] = (gate * dot(pick, grad_ref[...])).astype(BF16)


def combine_kernel(routes_ref, rows_ref, out_ref):
    tokens, width = out_ref.shape
    top = routes_ref.shape[1]
    count = rows_ref.shape[0]
    slots = slot_numbers(routes_ref)
    row = lax.broadcasted_iota(jnp.int32, (tokens, count), 0)
    col = lax.broadcasted_iota(jnp.int32, (tokens, count), 1)
    pick = jnp.zeros((tokens, count), F32)
    for r, slot in enumerate(slots):
        pick = jnp.where((col == slot) & (row == r // top), 1.0, pick)
    out_ref[...] = dot(pick.astype(BF16), rows_ref[...]).astype(BF16)


def expert_kernel(x_ref, wg_ref, wu_ref, wd_ref, out_ref):
    width = wg_ref.shape[1]
    x = x_ref[:, :width]
    grad = x_ref[:, width:]
    gate = dot(wg_ref[...], x, NT)
    up = dot(wu_ref[...], x, NT)
    hidden = dot(wd_ref[...], grad, NT)
    sigmoid = jax.nn.sigmoid(gate)
    grad_up = (hidden * gate * sigmoid).astype(BF16)
    grad_gate = (hidden * up * sigmoid * (1.0 + gate * (1.0 - sigmoid))).astype(BF16)
    out_ref[...] = (dot(grad_gate, wg_ref[...], TN) + dot(grad_up, wu_ref[...], TN)).astype(BF16)


def sum_kernel(in_ref, out_ref):
    total = in_ref[0].astype(F32)
    for part in range(1, in_ref.shape[0]):
        total = total + in_ref[part].astype(F32)
    out_ref[...] = total.astype(BF16)


SMEM = pl.BlockSpec(memory_space=pltpu.SMEM)
VMEM = pl.BlockSpec(memory_space=pltpu.VMEM)


def params(mib):
    return pltpu.CompilerParams(vmem_limit_bytes=mib << 20)


def cost(flops, moved):
    return pl.CostEstimate(flops=int(flops), bytes_accessed=int(moved), transcendentals=0)


def per_device(
    queries, keys, values, out_grad, log_decay, doc_lengths, moe_input, moe_grad,
    routes, gate_weights, w_gate, w_up, w_down,
):
    length, width_all = queries.shape[1:]
    heads = log_decay.shape[1]
    size = width_all // heads
    blocks = lax.axis_size("ctx")
    experts = lax.axis_size("exp")
    tokens, width = moe_input.shape
    slots = 2 * experts
    place = lax.axis_index("ctx").astype(jnp.int32).reshape(1)
    q, k, v, g = queries[0], keys[0], values[0], out_grad[0]
    logs = log_decay[0]

    filled = pl.pallas_call(
        fill_kernel,
        out_shape=jax.ShapeDtypeStruct((slots, 2 * width), BF16),
        in_specs=[SMEM, SMEM, VMEM, VMEM],
        out_specs=VMEM,
        compiler_params=params(16),
        cost_estimate=cost(4 * slots * tokens * width, 8 * slots * width),
        name="fill",
    )(routes, gate_weights, moe_input, moe_grad)
    arrived = lax.all_to_all(
        filled.reshape(experts, 2, 2 * width), "exp", split_axis=0, concat_axis=0, tiled=True
    ).reshape(slots, 2 * width)
    gathered = lax.all_gather(arrived, "ctx", axis=0, tiled=True)

    steps = heads // HEADS_STEP
    cols = HEADS_STEP * size
    pairs = HEADS_STEP // 2
    position_spec = pl.BlockSpec((length, cols), lambda i: (0, i))
    log_spec = pl.BlockSpec((HEADS_STEP, length), lambda i: (i, 0))
    sent_rows = 4 * size + DECAY_ROWS
    local = pl.pallas_call(
        local_kernel,
        grid=(steps,),
        out_shape=jax.ShapeDtypeStruct((heads // 2, sent_rows, size), BF16),
        in_specs=[SMEM, SMEM, log_spec] + [position_spec] * 4,
        out_specs=pl.BlockSpec((pairs, sent_rows, size), lambda i: (i, 0, 0)),
        compiler_params=params(24),
        cost_estimate=cost(4 * heads * length * size * size, 12 * length * width_all),
        name="local_sums",
    )(doc_lengths, place, logs, q, k, v, g)
    own_heads = lax.all_to_all(local, "ctx", split_axis=0, concat_axis=0, tiled=True)
    scanned = pl.pallas_call(
        scan_kernel,
        out_shape=jax.ShapeDtypeStruct((blocks, 4 * size, size), BF16),
        in_specs=[VMEM],
        out_specs=VMEM,
        compiler_params=params(24),
        cost_estimate=cost(blocks * 8 * size * size, 16 * blocks * size * size),
        name="scan",
    )(own_heads)
    states = lax.all_to_all(scanned, "ctx", split_axis=0, concat_axis=0, tiled=True)

    hidden = w_gate.shape[1]
    rows = blocks * slots
    row_step = rows // 2
    weight_spec = pl.BlockSpec((hidden, width), lambda i: (0, 0))
    term = pl.pallas_call(
        expert_kernel,
        grid=(rows // row_step,),
        out_shape=jax.ShapeDtypeStruct((rows, width), BF16),
        in_specs=[pl.BlockSpec((row_step, 2 * width), lambda i: (i, 0))] + [weight_spec] * 3,
        out_specs=pl.BlockSpec((row_step, width), lambda i: (i, 0)),
        compiler_params=params(48),
        cost_estimate=cost(10 * rows * hidden * width, 2 * width * (3 * rows + 3 * hidden)),
        name="experts",
    )(gathered, w_gate[0], w_up[0], w_down[0])
    spread = lax.all_to_all(
        term.reshape(blocks, slots, width), "ctx", split_axis=0, concat_axis=0, tiled=True
    )
    summed = pl.pallas_call(
        sum_kernel,
        out_shape=jax.ShapeDtypeStruct((slots, width), BF16),
        in_specs=[VMEM],
        out_specs=VMEM,
        compiler_params=params(24),
        cost_estimate=cost(blocks * slots * width, 2 * (blocks + 1) * slots * width),
        name="sum_slices",
    )(spread)
    returned = lax.all_to_all(
        summed.reshape(experts, 2, width), "exp", split_axis=0, concat_axis=0, tiled=True
    ).reshape(slots, width)
    d_moe = pl.pallas_call(
        combine_kernel,
        out_shape=jax.ShapeDtypeStruct((tokens, width), BF16),
        in_specs=[SMEM, VMEM],
        out_specs=VMEM,
        compiler_params=params(16),
        cost_estimate=cost(2 * slots * tokens * width, 4 * slots * width),
        name="combine",
    )(routes, returned)

    grad_q, grad_k, grad_v = pl.pallas_call(
        grads_kernel,
        grid=(steps,),
        out_shape=[jax.ShapeDtypeStruct((length, width_all), BF16)] * 3,
        in_specs=[SMEM, SMEM, log_spec]
        + [position_spec] * 4
        + [pl.BlockSpec((pairs, 4 * size, size), lambda i: (i, 0, 0))],
        out_specs=[position_spec] * 3,
        compiler_params=params(32),
        cost_estimate=cost(16 * heads * length * size * size, 18 * length * width_all),
        name="attention_grads",
    )(doc_lengths, place, logs, q, k, v, g, states)
    return (grad_q[None], grad_k[None], grad_v[None], d_moe)


def solution(mesh):
    rows = P("exp", "ctx", None)
    tokens = P(("ctx", "exp"), None)
    return jax.shard_map(
        per_device,
        mesh=mesh,
        in_specs=(rows, rows, rows, rows, P("exp", None, "ctx"), P("exp", None))
        + (tokens,) * 4
        + (rows,) * 3,
        out_specs=(rows, rows, rows, tokens),
        check_vma=False,
    )
```

```python
import functools

import jax
import jax.numpy as jnp
from jax import lax
from jax.experimental import pallas as pl
from jax.experimental.pallas import tpu as pltpu
from jax.sharding import PartitionSpec as P

F32 = jnp.float32
BF16 = jnp.bfloat16
NT = (((1,), (1,)), ((), ()))
TN = (((0,), (0,)), ((), ()))
HEADS_STEP = 8
DECAY_ROWS = 16
VMEM_MIB = 60
SIDE = 4
HALF = 16
NEAR = (0, -1, 1, 2)


def dot(a, b, dims=(((1,), (0,)), ((), ()))):
    return lax.dot_general(a, b, dims, preferred_element_type=F32)


def exact_dot(a, b, dims=(((1,), (0,)), ((), ()))):
    return lax.dot_general(
        a, b, dims, precision=lax.Precision.HIGHEST, preferred_element_type=F32
    )


def segments(lengths_ref, place_ref, length, axis):
    shape = (length, 1) if axis == 0 else (1, length)
    base = place_ref[0] * length
    at = lax.broadcasted_iota(jnp.int32, shape, axis) + base
    count = jnp.zeros(shape, jnp.int32)
    start = jnp.int32(0)
    for doc in range(lengths_ref.shape[1]):
        inside = jnp.where(start >= base, 1, 0)
        count = count + jnp.where(at >= start, inside, 0)
        start = start + lengths_ref[0, doc]
    last = jnp.int32(0)
    start = jnp.int32(0)
    for doc in range(lengths_ref.shape[1]):
        last = last + jnp.where((start >= base) & (start < base + length), 1, 0)
        start = start + lengths_ref[0, doc]
    return count, last


def running_sums(log_ref, length):
    logs = log_ref[...]
    low = lax.broadcasted_iota(jnp.int32, (length, length), 0)
    high = lax.broadcasted_iota(jnp.int32, (length, length), 1)
    upper = jnp.where(low <= high, 1.0, 0.0).astype(F32)
    rows = exact_dot(logs, upper)
    return rows, rows.T


def local_kernel(lengths_ref, place_ref, log_ref, q_ref, k_ref, v_ref, g_ref, out_ref):
    length = q_ref.shape[0]
    size = q_ref.shape[1] // HEADS_STEP
    seg, last = segments(lengths_ref, place_ref, length, 0)
    rows, cols = running_sums(log_ref, length)
    first_doc = jnp.where(seg == 0, 1.0, 0.0).astype(F32)
    last_doc = jnp.where(seg == last, 1.0, 0.0).astype(F32)
    whole = jnp.where(last == 0, 1.0, 0.0).astype(F32)
    row_id = lax.broadcasted_iota(jnp.int32, (DECAY_ROWS, size), 0)
    for pair in range(HEADS_STEP // 2):
        pieces = jnp.zeros((DECAY_ROWS, size), F32)
        for own in range(2):
            head = 2 * pair + own
            at = slice(head * size, (head + 1) * size)
            col = cols[:, head : head + 1]
            end = cols[length - 1 : length, head : head + 1]
            from_start = jnp.exp(col) * first_doc
            to_end = jnp.exp(end - col) * last_doc
            keys_end = (k_ref[:, at].astype(F32) * to_end).astype(BF16)
            queries_start = (q_ref[:, at].astype(F32) * from_start).astype(BF16)
            out_ref[pair, own * size : (own + 1) * size, :] = dot(
                keys_end, v_ref[:, at], TN
            ).astype(BF16)
            out_ref[pair, (2 + own) * size : (3 + own) * size, :] = dot(
                queries_start, g_ref[:, at], TN
            ).astype(BF16)
            rest = jnp.broadcast_to(jnp.exp(end) * whole, (DECAY_ROWS, size))
            for part in range(3):
                piece = rest.astype(BF16).astype(F32)
                pieces = jnp.where(row_id == own * 8 + part, piece, pieces)
                rest = rest - piece
        out_ref[pair, 4 * size :, :] = pieces.astype(BF16)


def scan_kernel(decay_ref, in_ref, out_ref):
    blocks, size = in_ref.shape[:2]
    step = pl.program_id(0)

    def run(own, order):
        carry = jnp.zeros((size, size), F32)
        for block in order:
            out_ref[block] = carry.astype(BF16)
            rows = decay_ref[block].astype(F32)[own * 8 : own * 8 + 3]
            decay = rows[0:1] + rows[1:2] + rows[2:3]
            carry = decay * carry + in_ref[block].astype(F32)

    for own in range(2):
        for kind in range(2):
            order = range(blocks) if kind == 0 else range(blocks - 1, -1, -1)

            @pl.when(step == 2 * kind + own)
            def _(own=own, order=order):
                run(own, order)


def grads_kernel(
    lengths_ref, place_ref, log_ref, q_ref, k_ref, v_ref, g_ref, s_ref, dq_ref, dk_ref, dv_ref
):
    length = q_ref.shape[0]
    size = q_ref.shape[1] // HEADS_STEP
    seg, last = segments(lengths_ref, place_ref, length, 0)
    seg_row, _ = segments(lengths_ref, place_ref, length, 1)
    rows, cols = running_sums(log_ref, length)
    first_doc = jnp.where(seg == 0, 1.0, 0.0).astype(F32)
    last_doc = jnp.where(seg == last, 1.0, 0.0).astype(F32)
    low = lax.broadcasted_iota(jnp.int32, (length, length), 0)
    high = lax.broadcasted_iota(jnp.int32, (length, length), 1)
    linked = (low >= high) & (seg == seg_row)
    for head in range(HEADS_STEP):
        at = slice(head * size, (head + 1) * size)
        pair, own = head // 2, head % 2
        col = cols[:, head : head + 1]
        end = cols[length - 1 : length, head : head + 1]
        from_start = jnp.exp(col) * first_doc
        to_end = jnp.exp(end - col) * last_doc
        within = jnp.exp(jnp.where(linked, col - rows[head : head + 1, :], -1e9))
        q, k, v, g = q_ref[:, at], k_ref[:, at], v_ref[:, at], g_ref[:, at]
        state = s_ref[pair, own * size : (own + 1) * size, :]
        carried = s_ref[pair, (2 + own) * size : (3 + own) * size, :]
        weight_q = (dot(g, v, NT) * within).astype(BF16)
        weight_v = (dot(q, k, NT) * within).astype(BF16)
        dq_ref[:, at] = (dot(weight_q, k) + from_start * dot(g, state, NT)).astype(BF16)
        dk_ref[:, at] = (dot(weight_q, q, TN) + to_end * dot(v, carried, NT)).astype(BF16)
        dv_ref[:, at] = (dot(weight_v, g, TN) + to_end * dot(k, carried)).astype(BF16)


def slot_numbers(routes_ref):
    top, tokens = routes_ref.shape
    flat = [routes_ref[k, i] for i in range(tokens) for k in range(top)]
    slots = []
    for r, expert in enumerate(flat):
        rank = jnp.int32(0)
        for earlier in flat[:r]:
            rank = rank + jnp.where(earlier == expert, 1, 0)
        slots.append(2 * expert + rank)
    return slots


def fill_kernel(routes_ref, gates_ref, in_ref, grad_ref, out_ref):
    tokens, width = in_ref.shape
    top = routes_ref.shape[0]
    count = 2 * out_ref.shape[0]
    slots = slot_numbers(routes_ref)
    row = lax.broadcasted_iota(jnp.int32, (count, tokens), 0)
    col = lax.broadcasted_iota(jnp.int32, (count, tokens), 1)
    row_one = lax.broadcasted_iota(jnp.int32, (count, 1), 0)
    pick = jnp.zeros((count, tokens), F32)
    gate = jnp.zeros((count, 1), F32)
    for r, slot in enumerate(slots):
        pick = jnp.where((row == slot) & (col == r // top), 1.0, pick)
        gate = jnp.where(row_one == slot, gates_ref[r % top, r // top], gate)
    pick = pick.astype(BF16)
    rows = dot(pick, in_ref[...]).astype(BF16)
    grads = (gate * dot(pick, grad_ref[...])).astype(BF16)
    for expert in range(out_ref.shape[0]):
        own = slice(2 * expert, 2 * expert + 2)
        out_ref[expert, :, :width] = rows[own]
        out_ref[expert, :, width:] = grads[own]


def combine_kernel(routes_ref, rows_ref, out_ref):
    tokens, width = out_ref.shape
    top = routes_ref.shape[0]
    count = rows_ref.shape[0]
    slots = slot_numbers(routes_ref)
    row = lax.broadcasted_iota(jnp.int32, (tokens, count), 0)
    col = lax.broadcasted_iota(jnp.int32, (tokens, count), 1)
    pick = jnp.zeros((tokens, count), F32)
    for r, slot in enumerate(slots):
        pick = jnp.where((col == slot) & (row == r // top), 1.0, pick)
    out_ref[...] = dot(pick.astype(BF16), rows_ref[...]).astype(BF16)


def expert_kernel(count, *refs):
    buffers, weights = refs[:count], refs[count : count + 3]
    outs = refs[count + 3 : 2 * count + 3]
    x_ref, wg_ref, wu_ref, wd_ref, x_sem, w_sem = refs[2 * count + 3 :]
    copies = []
    at = 0
    for n, buffer in enumerate(buffers):
        rows = buffer.shape[0]
        copies.append(pltpu.make_async_copy(buffer, x_ref.at[pl.ds(at, rows)], x_sem.at[n]))
        at += rows
    loads = [
        pltpu.make_async_copy(weight, held, w_sem.at[n])
        for n, (weight, held) in enumerate(zip(weights, (wg_ref, wu_ref, wd_ref)))
    ]
    for copy in copies + loads:
        copy.start()
    for copy in copies:
        copy.wait()
    width = wg_ref.shape[1]
    loads[0].wait()
    gate = dot(wg_ref[...], x_ref[:, :width], NT)
    sigmoid = jax.nn.sigmoid(gate)
    loads[1].wait()
    up = dot(wu_ref[...], x_ref[:, :width], NT)
    loads[2].wait()
    hidden = dot(wd_ref[...], x_ref[:, width:], NT)
    grad_up = (hidden * gate * sigmoid).astype(BF16)
    grad_gate = (hidden * up * sigmoid * (1.0 + gate * (1.0 - sigmoid))).astype(BF16)
    term = (dot(grad_gate, wg_ref[...], TN) + dot(grad_up, wu_ref[...], TN)).astype(BF16)
    at = 0
    for out in outs:
        rows = out.shape[0]
        out[...] = term[at : at + rows]
        at += rows


def expert_rows(buffers, weights):
    count = len(buffers)
    hidden, width = weights[0].shape
    rows = sum(buffer.shape[0] for buffer in buffers)
    any_spec = pl.BlockSpec(memory_space=pl.ANY)
    return pl.pallas_call(
        functools.partial(expert_kernel, count),
        out_shape=[jax.ShapeDtypeStruct((buffer.shape[0], width), BF16) for buffer in buffers],
        in_specs=[any_spec] * (count + 3),
        out_specs=[VMEM] * count,
        scratch_shapes=[pltpu.VMEM((rows, 2 * width), BF16)]
        + [pltpu.VMEM((hidden, width), BF16)] * 3
        + [pltpu.SemaphoreType.DMA((count,)), pltpu.SemaphoreType.DMA((3,))],
        compiler_params=params(VMEM_MIB),
        cost_estimate=cost(10 * rows * hidden * width, 2 * width * (3 * rows + 3 * hidden)),
        name="experts",
    )(*buffers, *weights)


def add_kernel(count, *refs):
    parts, arrived, outs = refs[:count], refs[count : 2 * count], refs[2 * count :]
    for n, (part, more, out) in enumerate(zip(parts, arrived, outs)):
        cut = more.shape[0]
        at = slice(0, cut) if n % 2 == 0 else slice(cut, 2 * cut)
        rest = slice(cut, 2 * cut) if n % 2 == 0 else slice(0, cut)
        out[at, :] = (part[at, :].astype(F32) + more[...].astype(F32)).astype(BF16)
        out[rest, :] = part[rest, :]


def add_halves(parts, arrived):
    count = len(parts)
    return pl.pallas_call(
        functools.partial(add_kernel, count),
        out_shape=[jax.ShapeDtypeStruct(part.shape, BF16) for part in parts],
        in_specs=[VMEM] * (2 * count),
        out_specs=[VMEM] * count,
        compiler_params=params(VMEM_MIB),
        cost_estimate=cost(count * parts[0].size, 6 * count * parts[0].size),
        name="add_halves",
    )(*parts, *arrived)


def own_kernel(group, *refs):
    groups = len(refs) // (group + len(NEAR))
    ins, outs = refs[: groups * group], refs[groups * group :]
    for n in range(groups):
        total = ins[n * group][...].astype(F32)
        for ref in ins[n * group + 1 : (n + 1) * group]:
            total = total + ref[...].astype(F32)
        total = total.astype(BF16)
        for piece in range(len(NEAR)):
            outs[n * len(NEAR) + piece][...] = total[piece * HALF : (piece + 1) * HALF]


def add_own(groups):
    group = len(groups[0])
    width = groups[0][0].shape[1]
    count = len(groups) * len(NEAR)
    outs = pl.pallas_call(
        functools.partial(own_kernel, group),
        out_shape=[jax.ShapeDtypeStruct((HALF, width), BF16)] * count,
        in_specs=[VMEM] * (group * len(groups)),
        out_specs=[VMEM] * count,
        compiler_params=params(VMEM_MIB),
        cost_estimate=cost(count * HALF * width * group, 2 * count * HALF * width * group),
        name="add_own",
    )(*[ref for refs in groups for ref in refs])
    return [list(outs[n * len(NEAR) : (n + 1) * len(NEAR)]) for n in range(len(groups))]


def last_kernel(group, *refs):
    out_ref = refs[-1]
    for n in range(2):
        ins = refs[n * group : (n + 1) * group]
        total = ins[0][...].astype(F32)
        for ref in ins[1:]:
            total = total + ref[...].astype(F32)
        total = total.astype(BF16)
        for expert in range(HALF // 2):
            out_ref[n * HALF // 2 + expert] = total[2 * expert : 2 * expert + 2]


def add_last(first, second):
    width = first[0].shape[1]
    return pl.pallas_call(
        functools.partial(last_kernel, len(first)),
        out_shape=jax.ShapeDtypeStruct((HALF, 2, width), BF16),
        in_specs=[VMEM] * (2 * len(first)),
        out_specs=VMEM,
        compiler_params=params(VMEM_MIB),
        cost_estimate=cost(8 * HALF * width, 20 * HALF * width),
        name="add_last",
    )(*first, *second)


def along_x(step):
    return [(SIDE * y + x, SIDE * y + (x + step) % SIDE) for y in range(SIDE) for x in range(SIDE)]


def along_y(step):
    return [(SIDE * y + x, SIDE * ((y + step) % SIDE) + x) for y in range(SIDE) for x in range(SIDE)]


def send(array, pairs):
    return lax.ppermute(array, "ctx", pairs)


SMEM = pl.BlockSpec(memory_space=pltpu.SMEM)
VMEM = pl.BlockSpec(memory_space=pltpu.VMEM)


def params(mib):
    return pltpu.CompilerParams(vmem_limit_bytes=mib << 20)


def cost(flops, moved):
    return pl.CostEstimate(flops=int(flops), bytes_accessed=int(moved), transcendentals=0)


def per_device(
    queries, keys, values, out_grad, log_decay, doc_lengths, moe_input, moe_grad,
    routes, gate_weights, w_gate, w_up, w_down,
):
    length, width_all = queries.shape[1:]
    heads = log_decay.shape[1]
    size = width_all // heads
    blocks = lax.axis_size("ctx")
    experts = lax.axis_size("exp")
    tokens, width = moe_input.shape
    slots = 2 * experts
    place = lax.axis_index("ctx").astype(jnp.int32).reshape(1)
    q, k, v, g = queries[0], keys[0], values[0], out_grad[0]
    logs = log_decay[0]

    filled = pl.pallas_call(
        fill_kernel,
        out_shape=jax.ShapeDtypeStruct((experts, 2, 2 * width), BF16),
        in_specs=[SMEM, SMEM, VMEM, VMEM],
        out_specs=VMEM,
        compiler_params=params(VMEM_MIB),
        cost_estimate=cost(4 * slots * tokens * width, 8 * slots * width),
        name="fill",
    )(routes.T, gate_weights.T, moe_input, moe_grad)
    arrived = lax.all_to_all(
        filled, "exp", split_axis=0, concat_axis=0, tiled=True
    ).reshape(slots, 2 * width)

    logs, filled = lax.optimization_barrier((logs, filled))
    steps = heads // HEADS_STEP
    cols = HEADS_STEP * size
    pairs = HEADS_STEP // 2
    position_spec = pl.BlockSpec((length, cols), lambda i: (0, i))
    log_spec = pl.BlockSpec((HEADS_STEP, length), lambda i: (i, 0))
    sent_rows = 4 * size + DECAY_ROWS
    local = pl.pallas_call(
        local_kernel,
        grid=(steps,),
        out_shape=jax.ShapeDtypeStruct((heads // 2, sent_rows, size), BF16),
        in_specs=[SMEM, SMEM, log_spec] + [position_spec] * 4,
        out_specs=pl.BlockSpec((pairs, sent_rows, size), lambda i: (i, 0, 0)),
        compiler_params=params(VMEM_MIB),
        cost_estimate=cost(4 * heads * length * size * size, 12 * length * width_all),
        name="local_sums",
    )(doc_lengths, place, logs, q, k, v, g)
    arrived, _ = lax.optimization_barrier((arrived, local))

    first, second = arrived[:HALF], arrived[HALF:]
    first_near = [first] + [send(first, along_x(-d)) for d in NEAR[1:]]
    second_near = [second] + [send(second, along_y(-d)) for d in NEAR[1:]]
    first_row = jnp.concatenate(first_near)
    second_col = jnp.concatenate(second_near)
    weights = (w_gate[0], w_up[0], w_down[0])
    first_up, first_down = send(first_row, along_y(1)), send(first_row, along_y(-1))
    second_left, second_right = send(second_col, along_x(1)), send(second_col, along_x(-1))
    first_own, second_own = expert_rows([first_row, second_col], weights)
    held = lax.optimization_barrier(
        (first_up, first_down, second_left, second_right, first_own, second_own, local)
    )
    first_up, first_down, second_left, second_right, first_own, second_own, local = held

    own_heads = lax.all_to_all(local, "ctx", split_axis=0, concat_axis=0, tiled=True)
    state_spec = pl.BlockSpec((blocks, size, size), lambda i: (0, i, 0))
    scanned = pl.pallas_call(
        scan_kernel,
        grid=(4,),
        out_shape=jax.ShapeDtypeStruct((blocks, 4 * size, size), BF16),
        in_specs=[
            pl.BlockSpec((blocks, DECAY_ROWS, size), lambda i: (0, 4 * size // DECAY_ROWS, 0)),
            state_spec,
        ],
        out_specs=state_spec,
        compiler_params=params(VMEM_MIB),
        cost_estimate=cost(blocks * 8 * size * size, 16 * blocks * size * size),
        name="scan",
    )(own_heads, own_heads)

    cut = 2 * HALF
    far = [
        send(first_up[:cut], along_y(1)), send(first_down[cut:], along_y(-1)),
        send(second_left[:cut], along_x(1)), send(second_right[cut:], along_x(-1)),
    ]
    near_terms = expert_rows([first_up, first_down, second_left, second_right], weights)
    far_terms = expert_rows(far, weights)
    ways = [along_y(1), along_y(-1), along_x(1), along_x(-1)]
    arrived_far = [send(part, way) for part, way in zip(far_terms, ways)]
    up, down, left, right = near_terms
    *arrived_far, scanned = lax.optimization_barrier((*arrived_far, scanned))
    states = lax.all_to_all(scanned, "ctx", split_axis=0, concat_axis=0, tiled=True)
    halves = add_halves([down, up, right, left], arrived_far)
    arrived_near = [send(part, way) for part, way in zip(halves, ways)]
    first_sum, second_sum = add_own(
        [[first_own] + arrived_near[:2], [second_own] + arrived_near[2:]]
    )
    first_sum[0], states = lax.optimization_barrier((first_sum[0], states))
    summed = add_last(
        first_sum[:1] + [send(part, along_x(d)) for part, d in zip(first_sum[1:], NEAR[1:])],
        second_sum[:1] + [send(part, along_y(d)) for part, d in zip(second_sum[1:], NEAR[1:])],
    )
    returned = lax.all_to_all(
        summed, "exp", split_axis=0, concat_axis=0, tiled=True
    ).reshape(slots, width)
    d_moe = pl.pallas_call(
        combine_kernel,
        out_shape=jax.ShapeDtypeStruct((tokens, width), BF16),
        in_specs=[SMEM, VMEM],
        out_specs=VMEM,
        compiler_params=params(VMEM_MIB),
        cost_estimate=cost(2 * slots * tokens * width, 4 * slots * width),
        name="combine",
    )(routes.T, returned)

    grad_q, grad_k, grad_v = pl.pallas_call(
        grads_kernel,
        grid=(steps,),
        out_shape=[jax.ShapeDtypeStruct((length, width_all), BF16)] * 3,
        in_specs=[SMEM, SMEM, log_spec]
        + [position_spec] * 4
        + [pl.BlockSpec((pairs, 4 * size, size), lambda i: (i, 0, 0))],
        out_specs=[position_spec] * 3,
        compiler_params=params(VMEM_MIB),
        cost_estimate=cost(16 * heads * length * size * size, 18 * length * width_all),
        name="attention_grads",
    )(doc_lengths, place, logs, q, k, v, g, states)
    return (grad_q[None], grad_k[None], grad_v[None], d_moe)


def solution(mesh):
    rows = P("exp", "ctx", None)
    tokens = P(("ctx", "exp"), None)
    return jax.shard_map(
        per_device,
        mesh=mesh,
        in_specs=(rows, rows, rows, rows, P("exp", None, "ctx"), P("exp", None))
        + (tokens,) * 4
        + (rows,) * 3,
        out_specs=(rows, rows, rows, tokens),
        check_vma=False,
    )
```

```python
import functools

import jax
import jax.numpy as jnp
from jax import lax
from jax.experimental import pallas as pl
from jax.experimental.pallas import tpu as pltpu
from jax.sharding import PartitionSpec as P

F32 = jnp.float32
BF16 = jnp.bfloat16
NT = (((1,), (1,)), ((), ()))
TN = (((0,), (0,)), ((), ()))
HEADS_STEP = 8
DECAY_ROWS = 16
VMEM_MIB = 60
SMALL_MIB = 16
SIDE = 4
HALF = 16
NEAR = (0, -1, 1, 2)


def dot(a, b, dims=(((1,), (0,)), ((), ()))):
    return lax.dot_general(a, b, dims, preferred_element_type=F32)


def exact_dot(a, b, dims=(((1,), (0,)), ((), ()))):
    return lax.dot_general(
        a, b, dims, precision=lax.Precision.HIGHEST, preferred_element_type=F32
    )


def segments(lengths_ref, place_ref, length, axis):
    shape = (length, 1) if axis == 0 else (1, length)
    base = place_ref[0] * length
    at = lax.broadcasted_iota(jnp.int32, shape, axis) + base
    count = jnp.zeros(shape, jnp.int32)
    start = jnp.int32(0)
    for doc in range(lengths_ref.shape[1]):
        inside = jnp.where(start >= base, 1, 0)
        count = count + jnp.where(at >= start, inside, 0)
        start = start + lengths_ref[0, doc]
    last = jnp.int32(0)
    start = jnp.int32(0)
    for doc in range(lengths_ref.shape[1]):
        last = last + jnp.where((start >= base) & (start < base + length), 1, 0)
        start = start + lengths_ref[0, doc]
    return count, last


def running_sums(log_ref, length):
    logs = log_ref[...]
    low = lax.broadcasted_iota(jnp.int32, (length, length), 0)
    high = lax.broadcasted_iota(jnp.int32, (length, length), 1)
    upper = jnp.where(low <= high, 1.0, 0.0).astype(F32)
    rows = exact_dot(logs, upper)
    return rows, rows.T


def local_kernel(lengths_ref, place_ref, log_ref, q_ref, k_ref, v_ref, g_ref, out_ref):
    length = q_ref.shape[0]
    size = q_ref.shape[1] // HEADS_STEP
    seg, last = segments(lengths_ref, place_ref, length, 0)
    rows, cols = running_sums(log_ref, length)
    first_doc = jnp.where(seg == 0, 1.0, 0.0).astype(F32)
    last_doc = jnp.where(seg == last, 1.0, 0.0).astype(F32)
    whole = jnp.where(last == 0, 1.0, 0.0).astype(F32)
    row_id = lax.broadcasted_iota(jnp.int32, (DECAY_ROWS, size), 0)
    for pair in range(HEADS_STEP // 2):
        pieces = jnp.zeros((DECAY_ROWS, size), F32)
        for own in range(2):
            head = 2 * pair + own
            at = slice(head * size, (head + 1) * size)
            col = cols[:, head : head + 1]
            end = cols[length - 1 : length, head : head + 1]
            from_start = jnp.exp(col) * first_doc
            to_end = jnp.exp(end - col) * last_doc
            keys_end = (k_ref[:, at].astype(F32) * to_end).astype(BF16)
            queries_start = (q_ref[:, at].astype(F32) * from_start).astype(BF16)
            out_ref[pair, own * size : (own + 1) * size, :] = dot(
                keys_end, v_ref[:, at], TN
            ).astype(BF16)
            out_ref[pair, (2 + own) * size : (3 + own) * size, :] = dot(
                queries_start, g_ref[:, at], TN
            ).astype(BF16)
            rest = jnp.broadcast_to(jnp.exp(end) * whole, (DECAY_ROWS, size))
            for part in range(3):
                piece = rest.astype(BF16).astype(F32)
                pieces = jnp.where(row_id == own * 8 + part, piece, pieces)
                rest = rest - piece
        out_ref[pair, 4 * size :, :] = pieces.astype(BF16)


def scan_kernel(decay_ref, in_ref, out_ref):
    blocks, size = in_ref.shape[:2]
    step = pl.program_id(0)

    def run(own, order):
        carry = jnp.zeros((size, size), F32)
        for block in order:
            out_ref[block] = carry.astype(BF16)
            rows = decay_ref[block].astype(F32)[own * 8 : own * 8 + 3]
            decay = rows[0:1] + rows[1:2] + rows[2:3]
            carry = decay * carry + in_ref[block].astype(F32)

    for own in range(2):
        for kind in range(2):
            order = range(blocks) if kind == 0 else range(blocks - 1, -1, -1)

            @pl.when(step == 2 * kind + own)
            def _(own=own, order=order):
                run(own, order)


def grads_kernel(
    lengths_ref, place_ref, log_ref, q_ref, k_ref, v_ref, g_ref, s_ref, dq_ref, dk_ref, dv_ref
):
    length = q_ref.shape[0]
    size = q_ref.shape[1] // HEADS_STEP
    seg, last = segments(lengths_ref, place_ref, length, 0)
    seg_row, _ = segments(lengths_ref, place_ref, length, 1)
    rows, cols = running_sums(log_ref, length)
    first_doc = jnp.where(seg == 0, 1.0, 0.0).astype(F32)
    last_doc = jnp.where(seg == last, 1.0, 0.0).astype(F32)
    low = lax.broadcasted_iota(jnp.int32, (length, length), 0)
    high = lax.broadcasted_iota(jnp.int32, (length, length), 1)
    linked = (low >= high) & (seg == seg_row)
    for head in range(HEADS_STEP):
        at = slice(head * size, (head + 1) * size)
        pair, own = head // 2, head % 2
        col = cols[:, head : head + 1]
        end = cols[length - 1 : length, head : head + 1]
        from_start = jnp.exp(col) * first_doc
        to_end = jnp.exp(end - col) * last_doc
        within = jnp.exp(jnp.where(linked, col - rows[head : head + 1, :], -1e9))
        q, k, v, g = q_ref[:, at], k_ref[:, at], v_ref[:, at], g_ref[:, at]
        state = s_ref[pair, own * size : (own + 1) * size, :]
        carried = s_ref[pair, (2 + own) * size : (3 + own) * size, :]
        weight_q = (dot(g, v, NT) * within).astype(BF16)
        weight_v = (dot(q, k, NT) * within).astype(BF16)
        dq_ref[:, at] = (dot(weight_q, k) + from_start * dot(g, state, NT)).astype(BF16)
        dk_ref[:, at] = (dot(weight_q, q, TN) + to_end * dot(v, carried, NT)).astype(BF16)
        dv_ref[:, at] = (dot(weight_v, g, TN) + to_end * dot(k, carried)).astype(BF16)


def slot_numbers(routes_ref):
    top, tokens = routes_ref.shape
    flat = [routes_ref[k, i] for i in range(tokens) for k in range(top)]
    slots = []
    for r, expert in enumerate(flat):
        rank = jnp.int32(0)
        for earlier in flat[:r]:
            rank = rank + jnp.where(earlier == expert, 1, 0)
        slots.append(2 * expert + rank)
    return slots


def fill_kernel(routes_ref, gates_ref, in_ref, grad_ref, out_ref):
    tokens, width = in_ref.shape
    top = routes_ref.shape[0]
    count = 2 * out_ref.shape[0]
    slots = slot_numbers(routes_ref)
    row = lax.broadcasted_iota(jnp.int32, (count, tokens), 0)
    col = lax.broadcasted_iota(jnp.int32, (count, tokens), 1)
    row_one = lax.broadcasted_iota(jnp.int32, (count, 1), 0)
    pick = jnp.zeros((count, tokens), F32)
    gate = jnp.zeros((count, 1), F32)
    for r, slot in enumerate(slots):
        pick = jnp.where((row == slot) & (col == r // top), 1.0, pick)
        gate = jnp.where(row_one == slot, gates_ref[r % top, r // top], gate)
    pick = pick.astype(BF16)
    rows = dot(pick, in_ref[...]).astype(BF16)
    grads = (gate * dot(pick, grad_ref[...])).astype(BF16)
    for expert in range(out_ref.shape[0]):
        own = slice(2 * expert, 2 * expert + 2)
        out_ref[expert, :, :width] = rows[own]
        out_ref[expert, :, width:] = grads[own]


def combine_kernel(routes_ref, rows_ref, out_ref):
    tokens, width = out_ref.shape
    top = routes_ref.shape[0]
    count = rows_ref.shape[0]
    slots = slot_numbers(routes_ref)
    row = lax.broadcasted_iota(jnp.int32, (tokens, count), 0)
    col = lax.broadcasted_iota(jnp.int32, (tokens, count), 1)
    pick = jnp.zeros((tokens, count), F32)
    for r, slot in enumerate(slots):
        pick = jnp.where((col == slot) & (row == r // top), 1.0, pick)
    out_ref[...] = dot(pick.astype(BF16), rows_ref[...]).astype(BF16)


def expert_kernel(count, *refs):
    buffers, weights = refs[:count], refs[count : count + 3]
    outs = refs[count + 3 : -6]
    x_ref, wg_ref, wu_ref, wd_ref, x_sem, w_sem = refs[-6:]
    copies = []
    at = 0
    for n, buffer in enumerate(buffers):
        rows = buffer.shape[0]
        copies.append(pltpu.make_async_copy(buffer, x_ref.at[pl.ds(at, rows)], x_sem.at[n]))
        at += rows
    loads = [
        pltpu.make_async_copy(weight, held, w_sem.at[n])
        for n, (weight, held) in enumerate(zip(weights, (wg_ref, wu_ref, wd_ref)))
    ]
    for copy in copies + loads:
        copy.start()
    for copy in copies:
        copy.wait()
    width = wg_ref.shape[1]
    loads[0].wait()
    gate = dot(wg_ref[...], x_ref[:, :width], NT)
    sigmoid = jax.nn.sigmoid(gate)
    loads[1].wait()
    up = dot(wu_ref[...], x_ref[:, :width], NT)
    loads[2].wait()
    hidden = dot(wd_ref[...], x_ref[:, width:], NT)
    grad_up = (hidden * gate * sigmoid).astype(BF16)
    grad_gate = (hidden * up * sigmoid * (1.0 + gate * (1.0 - sigmoid))).astype(BF16)
    term = (dot(grad_gate, wg_ref[...], TN) + dot(grad_up, wu_ref[...], TN)).astype(BF16)
    at = 0
    for out in outs:
        rows = out.shape[0]
        out[...] = term[at : at + rows]
        at += rows


def expert_rows(buffers, weights, outs=None):
    count = len(buffers)
    sizes = [buffer.shape[0] for buffer in buffers]
    sizes = sizes if outs is None else [sum(sizes) // outs] * outs
    hidden, width = weights[0].shape
    rows = sum(buffer.shape[0] for buffer in buffers)
    any_spec = pl.BlockSpec(memory_space=pl.ANY)
    return pl.pallas_call(
        functools.partial(expert_kernel, count),
        out_shape=[jax.ShapeDtypeStruct((size, width), BF16) for size in sizes],
        in_specs=[any_spec] * (count + 3),
        out_specs=[VMEM] * len(sizes),
        scratch_shapes=[pltpu.VMEM((rows, 2 * width), BF16)]
        + [pltpu.VMEM((hidden, width), BF16)] * 3
        + [pltpu.SemaphoreType.DMA((count,)), pltpu.SemaphoreType.DMA((3,))],
        compiler_params=params(VMEM_MIB),
        cost_estimate=cost(10 * rows * hidden * width, 2 * width * (3 * rows + 3 * hidden)),
        name="experts",
    )(*buffers, *weights)


def add_kernel(count, *refs):
    parts, arrived, outs = refs[:count], refs[count : 2 * count], refs[2 * count :]
    for n, (part, more, out) in enumerate(zip(parts, arrived, outs)):
        cut = more.shape[0]
        at = slice(0, cut) if n % 2 == 0 else slice(cut, 2 * cut)
        rest = slice(cut, 2 * cut) if n % 2 == 0 else slice(0, cut)
        out[at, :] = (part[at, :].astype(F32) + more[...].astype(F32)).astype(BF16)
        out[rest, :] = part[rest, :]


def add_halves(parts, arrived):
    count = len(parts)
    return pl.pallas_call(
        functools.partial(add_kernel, count),
        out_shape=[jax.ShapeDtypeStruct(part.shape, BF16) for part in parts],
        in_specs=[VMEM] * (2 * count),
        out_specs=[VMEM] * count,
        compiler_params=params(VMEM_MIB),
        cost_estimate=cost(count * parts[0].size, 6 * count * parts[0].size),
        name="add_halves",
    )(*parts, *arrived)


def own_kernel(group, *refs):
    groups = len(refs) // (group + len(NEAR))
    ins, outs = refs[: groups * group], refs[groups * group :]
    for n in range(groups):
        total = ins[n * group][...].astype(F32)
        for ref in ins[n * group + 1 : (n + 1) * group]:
            total = total + ref[...].astype(F32)
        total = total.astype(BF16)
        for piece in range(len(NEAR)):
            outs[n * len(NEAR) + piece][...] = total[piece * HALF : (piece + 1) * HALF]


def add_own(groups):
    group = len(groups[0])
    width = groups[0][0].shape[1]
    count = len(groups) * len(NEAR)
    outs = pl.pallas_call(
        functools.partial(own_kernel, group),
        out_shape=[jax.ShapeDtypeStruct((HALF, width), BF16)] * count,
        in_specs=[VMEM] * (group * len(groups)),
        out_specs=[VMEM] * count,
        compiler_params=params(SMALL_MIB),
        cost_estimate=cost(count * HALF * width * group, 2 * count * HALF * width * group),
        name="add_own",
    )(*[ref for refs in groups for ref in refs])
    return [list(outs[n * len(NEAR) : (n + 1) * len(NEAR)]) for n in range(len(groups))]


def last_kernel(group, *refs):
    out_ref = refs[-1]
    for n in range(2):
        ins = refs[n * group : (n + 1) * group]
        total = ins[0][...].astype(F32)
        for ref in ins[1:]:
            total = total + ref[...].astype(F32)
        total = total.astype(BF16)
        for expert in range(HALF // 2):
            out_ref[n * HALF // 2 + expert] = total[2 * expert : 2 * expert + 2]


def add_last(first, second):
    width = first[0].shape[1]
    return pl.pallas_call(
        functools.partial(last_kernel, len(first)),
        out_shape=jax.ShapeDtypeStruct((HALF, 2, width), BF16),
        in_specs=[VMEM] * (2 * len(first)),
        out_specs=VMEM,
        compiler_params=params(SMALL_MIB),
        cost_estimate=cost(8 * HALF * width, 20 * HALF * width),
        name="add_last",
    )(*first, *second)


def along_x(step):
    return [(SIDE * y + x, SIDE * y + (x + step) % SIDE) for y in range(SIDE) for x in range(SIDE)]


def along_y(step):
    return [(SIDE * y + x, SIDE * ((y + step) % SIDE) + x) for y in range(SIDE) for x in range(SIDE)]


def send(array, pairs):
    return lax.ppermute(array, "ctx", pairs)


SMEM = pl.BlockSpec(memory_space=pltpu.SMEM)
VMEM = pl.BlockSpec(memory_space=pltpu.VMEM)


def params(mib):
    return pltpu.CompilerParams(vmem_limit_bytes=mib << 20)


def cost(flops, moved):
    return pl.CostEstimate(flops=int(flops), bytes_accessed=int(moved), transcendentals=0)


def per_device(
    queries, keys, values, out_grad, log_decay, doc_lengths, moe_input, moe_grad,
    routes, gate_weights, w_gate, w_up, w_down,
):
    length, width_all = queries.shape[1:]
    heads = log_decay.shape[1]
    size = width_all // heads
    blocks = lax.axis_size("ctx")
    experts = lax.axis_size("exp")
    tokens, width = moe_input.shape
    slots = 2 * experts
    place = lax.axis_index("ctx").astype(jnp.int32).reshape(1)
    q, k, v, g = queries[0], keys[0], values[0], out_grad[0]
    logs = log_decay[0]

    filled = pl.pallas_call(
        fill_kernel,
        out_shape=jax.ShapeDtypeStruct((experts, 2, 2 * width), BF16),
        in_specs=[SMEM, SMEM, VMEM, VMEM],
        out_specs=VMEM,
        compiler_params=params(VMEM_MIB),
        cost_estimate=cost(4 * slots * tokens * width, 8 * slots * width),
        name="fill",
    )(routes.T, gate_weights.T, moe_input, moe_grad)
    arrived = lax.all_to_all(
        filled, "exp", split_axis=0, concat_axis=0, tiled=True
    ).reshape(slots, 2 * width)

    logs, filled = lax.optimization_barrier((logs, filled))
    steps = heads // HEADS_STEP
    cols = HEADS_STEP * size
    pairs = HEADS_STEP // 2
    position_spec = pl.BlockSpec((length, cols), lambda i: (0, i))
    log_spec = pl.BlockSpec((HEADS_STEP, length), lambda i: (i, 0))
    sent_rows = 4 * size + DECAY_ROWS
    local = pl.pallas_call(
        local_kernel,
        grid=(steps,),
        out_shape=jax.ShapeDtypeStruct((heads // 2, sent_rows, size), BF16),
        in_specs=[SMEM, SMEM, log_spec] + [position_spec] * 4,
        out_specs=pl.BlockSpec((pairs, sent_rows, size), lambda i: (i, 0, 0)),
        compiler_params=params(VMEM_MIB),
        cost_estimate=cost(4 * heads * length * size * size, 12 * length * width_all),
        name="local_sums",
    )(doc_lengths, place, logs, q, k, v, g)
    arrived, _ = lax.optimization_barrier((arrived, local))

    first, second = arrived[:HALF], arrived[HALF:]
    first_near = [first] + [send(first, along_x(-d)) for d in NEAR[1:]]
    second_near = [second] + [send(second, along_y(-d)) for d in NEAR[1:]]
    first_row = [jnp.concatenate(first_near[:2]), jnp.concatenate(first_near[2:])]
    second_col = [jnp.concatenate(second_near[:2]), jnp.concatenate(second_near[2:])]
    weights = (w_gate[0], w_up[0], w_down[0])
    ways = [along_y(1), along_y(-1), along_x(1), along_x(-1)]
    both = [first_row, first_row, second_col, second_col]
    early = [send(pair[n % 2], ways[n]) for n, pair in enumerate(both)]
    far = [send(part, way) for part, way in zip(early, ways)]
    late = [send(pair[1 - n % 2], ways[n]) for n, pair in enumerate(both)]
    held = lax.optimization_barrier((*late, *far, local))
    late, far, local = list(held[:4]), list(held[4:8]), held[8]
    near = [
        early[0], late[0], late[1], early[1],
        early[2], late[2], late[3], early[3],
    ]
    *near_terms, first_own, second_own = expert_rows(near + first_row + second_col, weights, 6)
    own_heads = lax.all_to_all(local, "ctx", split_axis=0, concat_axis=0, tiled=True)
    state_spec = pl.BlockSpec((blocks, size, size), lambda i: (0, i, 0))
    scanned = pl.pallas_call(
        scan_kernel,
        grid=(4,),
        out_shape=jax.ShapeDtypeStruct((blocks, 4 * size, size), BF16),
        in_specs=[
            pl.BlockSpec((blocks, DECAY_ROWS, size), lambda i: (0, 4 * size // DECAY_ROWS, 0)),
            state_spec,
        ],
        out_specs=state_spec,
        compiler_params=params(SMALL_MIB),
        cost_estimate=cost(blocks * 8 * size * size, 16 * blocks * size * size),
        name="scan",
    )(own_heads, own_heads)

    far_terms = expert_rows(far, weights)
    arrived_far = [send(part, way) for part, way in zip(far_terms, ways)]
    up, down, left, right = near_terms
    halves = add_halves([down, up, right, left], arrived_far)
    arrived_near = [send(part, way) for part, way in zip(halves, ways)]
    *arrived_near, scanned = lax.optimization_barrier((*arrived_near, scanned))
    states = lax.all_to_all(scanned, "ctx", split_axis=0, concat_axis=0, tiled=True)
    first_sum, second_sum = add_own(
        [[first_own] + arrived_near[:2], [second_own] + arrived_near[2:]]
    )
    first_sum[0], states = lax.optimization_barrier((first_sum[0], states))
    summed = add_last(
        first_sum[:1] + [send(part, along_x(d)) for part, d in zip(first_sum[1:], NEAR[1:])],
        second_sum[:1] + [send(part, along_y(d)) for part, d in zip(second_sum[1:], NEAR[1:])],
    )
    returned = lax.all_to_all(
        summed, "exp", split_axis=0, concat_axis=0, tiled=True
    ).reshape(slots, width)
    d_moe = pl.pallas_call(
        combine_kernel,
        out_shape=jax.ShapeDtypeStruct((tokens, width), BF16),
        in_specs=[SMEM, VMEM],
        out_specs=VMEM,
        compiler_params=params(SMALL_MIB),
        cost_estimate=cost(2 * slots * tokens * width, 4 * slots * width),
        name="combine",
    )(routes.T, returned)

    grad_q, grad_k, grad_v = pl.pallas_call(
        grads_kernel,
        grid=(steps,),
        out_shape=[jax.ShapeDtypeStruct((length, width_all), BF16)] * 3,
        in_specs=[SMEM, SMEM, log_spec]
        + [position_spec] * 4
        + [pl.BlockSpec((pairs, 4 * size, size), lambda i: (i, 0, 0))],
        out_specs=[position_spec] * 3,
        compiler_params=params(VMEM_MIB),
        cost_estimate=cost(16 * heads * length * size * size, 18 * length * width_all),
        name="attention_grads",
    )(doc_lengths, place, logs, q, k, v, g, states)
    return (grad_q[None], grad_k[None], grad_v[None], d_moe)


def solution(mesh):
    rows = P("exp", "ctx", None)
    tokens = P(("ctx", "exp"), None)
    return jax.shard_map(
        per_device,
        mesh=mesh,
        in_specs=(rows, rows, rows, rows, P("exp", None, "ctx"), P("exp", None))
        + (tokens,) * 4
        + (rows,) * 3,
        out_specs=(rows, rows, rows, tokens),
        check_vma=False,
    )
```

```python
import functools

import jax
import jax.numpy as jnp
from jax import lax
from jax.experimental import pallas as pl
from jax.experimental.pallas import tpu as pltpu
from jax.sharding import PartitionSpec as P

F32 = jnp.float32
BF16 = jnp.bfloat16
NT = (((1,), (1,)), ((), ()))
TN = (((0,), (0,)), ((), ()))
HEADS_STEP = 8
DECAY_ROWS = 16
VMEM_MIB = 60
SMALL_MIB = 16
SIDE = 4
HALF = 16
NEAR = (0, -1, 1, 2)


def dot(a, b, dims=(((1,), (0,)), ((), ()))):
    return lax.dot_general(a, b, dims, preferred_element_type=F32)


def exact_dot(a, b, dims=(((1,), (0,)), ((), ()))):
    return lax.dot_general(
        a, b, dims, precision=lax.Precision.HIGHEST, preferred_element_type=F32
    )


def segments(lengths_ref, place_ref, length, axis):
    shape = (length, 1) if axis == 0 else (1, length)
    base = place_ref[0] * length
    at = lax.broadcasted_iota(jnp.int32, shape, axis) + base
    count = jnp.zeros(shape, jnp.int32)
    start = jnp.int32(0)
    for doc in range(lengths_ref.shape[1]):
        inside = jnp.where(start >= base, 1, 0)
        count = count + jnp.where(at >= start, inside, 0)
        start = start + lengths_ref[0, doc]
    last = jnp.int32(0)
    start = jnp.int32(0)
    for doc in range(lengths_ref.shape[1]):
        last = last + jnp.where((start >= base) & (start < base + length), 1, 0)
        start = start + lengths_ref[0, doc]
    return count, last


def running_sums(log_ref, length):
    logs = log_ref[...]
    low = lax.broadcasted_iota(jnp.int32, (length, length), 0)
    high = lax.broadcasted_iota(jnp.int32, (length, length), 1)
    upper = jnp.where(low <= high, 1.0, 0.0).astype(F32)
    rows = exact_dot(logs, upper)
    return rows, rows.T


def local_kernel(lengths_ref, place_ref, log_ref, q_ref, k_ref, v_ref, g_ref, out_ref):
    length = q_ref.shape[0]
    size = q_ref.shape[1] // HEADS_STEP
    seg, last = segments(lengths_ref, place_ref, length, 0)
    rows, cols = running_sums(log_ref, length)
    first_doc = jnp.where(seg == 0, 1.0, 0.0).astype(F32)
    last_doc = jnp.where(seg == last, 1.0, 0.0).astype(F32)
    whole = jnp.where(last == 0, 1.0, 0.0).astype(F32)
    row_id = lax.broadcasted_iota(jnp.int32, (DECAY_ROWS, size), 0)
    for pair in range(HEADS_STEP // 2):
        pieces = jnp.zeros((DECAY_ROWS, size), F32)
        for own in range(2):
            head = 2 * pair + own
            at = slice(head * size, (head + 1) * size)
            col = cols[:, head : head + 1]
            end = cols[length - 1 : length, head : head + 1]
            from_start = jnp.exp(col) * first_doc
            to_end = jnp.exp(end - col) * last_doc
            keys_end = (k_ref[:, at].astype(F32) * to_end).astype(BF16)
            queries_start = (q_ref[:, at].astype(F32) * from_start).astype(BF16)
            out_ref[pair, own * size : (own + 1) * size, :] = dot(
                keys_end, v_ref[:, at], TN
            ).astype(BF16)
            out_ref[pair, (2 + own) * size : (3 + own) * size, :] = dot(
                queries_start, g_ref[:, at], TN
            ).astype(BF16)
            rest = jnp.broadcast_to(jnp.exp(end) * whole, (DECAY_ROWS, size))
            for part in range(3):
                piece = rest.astype(BF16).astype(F32)
                pieces = jnp.where(row_id == own * 8 + part, piece, pieces)
                rest = rest - piece
        out_ref[pair, 4 * size :, :] = pieces.astype(BF16)


def scan_kernel(decay_ref, in_ref, out_ref):
    blocks, size = in_ref.shape[:2]
    step = pl.program_id(0)

    def run(own, order):
        carry = jnp.zeros((size, size), F32)
        for block in order:
            out_ref[block] = carry.astype(BF16)
            rows = decay_ref[block].astype(F32)[own * 8 : own * 8 + 3]
            decay = rows[0:1] + rows[1:2] + rows[2:3]
            carry = decay * carry + in_ref[block].astype(F32)

    for own in range(2):
        for kind in range(2):
            order = range(blocks) if kind == 0 else range(blocks - 1, -1, -1)

            @pl.when(step == 2 * kind + own)
            def _(own=own, order=order):
                run(own, order)


def grads_kernel(
    lengths_ref, place_ref, log_ref, q_ref, k_ref, v_ref, g_ref, s_ref, dq_ref, dk_ref, dv_ref
):
    length = q_ref.shape[0]
    size = q_ref.shape[1] // HEADS_STEP
    seg, last = segments(lengths_ref, place_ref, length, 0)
    seg_row, _ = segments(lengths_ref, place_ref, length, 1)
    rows, cols = running_sums(log_ref, length)
    first_doc = jnp.where(seg == 0, 1.0, 0.0).astype(F32)
    last_doc = jnp.where(seg == last, 1.0, 0.0).astype(F32)
    low = lax.broadcasted_iota(jnp.int32, (length, length), 0)
    high = lax.broadcasted_iota(jnp.int32, (length, length), 1)
    linked = (low >= high) & (seg == seg_row)
    for head in range(HEADS_STEP):
        at = slice(head * size, (head + 1) * size)
        pair, own = head // 2, head % 2
        col = cols[:, head : head + 1]
        end = cols[length - 1 : length, head : head + 1]
        from_start = jnp.exp(col) * first_doc
        to_end = jnp.exp(end - col) * last_doc
        within = jnp.exp(jnp.where(linked, col - rows[head : head + 1, :], -1e9))
        q, k, v, g = q_ref[:, at], k_ref[:, at], v_ref[:, at], g_ref[:, at]
        state = s_ref[pair, own * size : (own + 1) * size, :]
        carried = s_ref[pair, (2 + own) * size : (3 + own) * size, :]
        weight_q = (dot(g, v, NT) * within).astype(BF16)
        weight_v = (dot(q, k, NT) * within).astype(BF16)
        dq_ref[:, at] = (dot(weight_q, k) + from_start * dot(g, state, NT)).astype(BF16)
        dk_ref[:, at] = (dot(weight_q, q, TN) + to_end * dot(v, carried, NT)).astype(BF16)
        dv_ref[:, at] = (dot(weight_v, g, TN) + to_end * dot(k, carried)).astype(BF16)


def slot_numbers(routes_ref):
    top, tokens = routes_ref.shape
    flat = [routes_ref[k, i] for i in range(tokens) for k in range(top)]
    slots = []
    for r, expert in enumerate(flat):
        rank = jnp.int32(0)
        for earlier in flat[:r]:
            rank = rank + jnp.where(earlier == expert, 1, 0)
        slots.append(2 * expert + rank)
    return slots


def fill_kernel(routes_ref, gates_ref, in_ref, grad_ref, out_ref):
    tokens, width = in_ref.shape
    top = routes_ref.shape[0]
    count = 2 * out_ref.shape[0]
    slots = slot_numbers(routes_ref)
    row = lax.broadcasted_iota(jnp.int32, (count, tokens), 0)
    col = lax.broadcasted_iota(jnp.int32, (count, tokens), 1)
    row_one = lax.broadcasted_iota(jnp.int32, (count, 1), 0)
    pick = jnp.zeros((count, tokens), F32)
    gate = jnp.zeros((count, 1), F32)
    for r, slot in enumerate(slots):
        pick = jnp.where((row == slot) & (col == r // top), 1.0, pick)
        gate = jnp.where(row_one == slot, gates_ref[r % top, r // top], gate)
    pick = pick.astype(BF16)
    rows = dot(pick, in_ref[...]).astype(BF16)
    grads = (gate * dot(pick, grad_ref[...])).astype(BF16)
    for expert in range(out_ref.shape[0]):
        own = slice(2 * expert, 2 * expert + 2)
        out_ref[expert, :, :width] = rows[own]
        out_ref[expert, :, width:] = grads[own]


def combine_kernel(routes_ref, rows_ref, out_ref):
    tokens, width = out_ref.shape
    top = routes_ref.shape[0]
    count = rows_ref.shape[0]
    slots = slot_numbers(routes_ref)
    row = lax.broadcasted_iota(jnp.int32, (tokens, count), 0)
    col = lax.broadcasted_iota(jnp.int32, (tokens, count), 1)
    pick = jnp.zeros((tokens, count), F32)
    for r, slot in enumerate(slots):
        pick = jnp.where((col == slot) & (row == r // top), 1.0, pick)
    out_ref[...] = dot(pick.astype(BF16), rows_ref[...]).astype(BF16)


def expert_kernel(count, *refs):
    buffers, weights = refs[:count], refs[count : count + 3]
    outs = refs[count + 3 : -5]
    x_ref, both_ref, wd_ref, x_sem, w_sem = refs[-5:]
    hidden_units = wd_ref.shape[0]
    copies = []
    at = 0
    for n, buffer in enumerate(buffers):
        rows = buffer.shape[0]
        copies.append(pltpu.make_async_copy(buffer, x_ref.at[pl.ds(at, rows)], x_sem.at[n]))
        at += rows
    places = (
        both_ref.at[pl.ds(0, hidden_units)], both_ref.at[pl.ds(hidden_units, hidden_units)], wd_ref
    )
    loads = [
        pltpu.make_async_copy(weight, held, w_sem.at[n])
        for n, (weight, held) in enumerate(zip(weights, places))
    ]
    for copy in copies + loads:
        copy.start()
    for copy in copies:
        copy.wait()
    width = wd_ref.shape[1]
    loads[0].wait()
    loads[1].wait()
    gate_up = dot(both_ref[...], x_ref[:, :width], NT)
    gate, up = gate_up[:hidden_units], gate_up[hidden_units:]
    sigmoid = jax.nn.sigmoid(gate)
    loads[2].wait()
    hidden = dot(wd_ref[...], x_ref[:, width:], NT)
    grad_up = (hidden * gate * sigmoid).astype(BF16)
    grad_gate = (hidden * up * sigmoid * (1.0 + gate * (1.0 - sigmoid))).astype(BF16)
    term = dot(jnp.concatenate([grad_gate, grad_up]), both_ref[...], TN).astype(BF16)
    at = 0
    for out in outs:
        rows = out.shape[0]
        out[...] = term[at : at + rows]
        at += rows


def expert_rows(buffers, weights, outs=None):
    count = len(buffers)
    sizes = [buffer.shape[0] for buffer in buffers]
    sizes = sizes if outs is None else [sum(sizes) // outs] * outs
    hidden, width = weights[0].shape
    rows = sum(buffer.shape[0] for buffer in buffers)
    any_spec = pl.BlockSpec(memory_space=pl.ANY)
    return pl.pallas_call(
        functools.partial(expert_kernel, count),
        out_shape=[jax.ShapeDtypeStruct((size, width), BF16) for size in sizes],
        in_specs=[any_spec] * (count + 3),
        out_specs=[VMEM] * len(sizes),
        scratch_shapes=[pltpu.VMEM((rows, 2 * width), BF16)]
        + [pltpu.VMEM((2 * hidden, width), BF16), pltpu.VMEM((hidden, width), BF16)]
        + [pltpu.SemaphoreType.DMA((count,)), pltpu.SemaphoreType.DMA((3,))],
        compiler_params=params(VMEM_MIB),
        cost_estimate=cost(10 * rows * hidden * width, 2 * width * (3 * rows + 3 * hidden)),
        name="experts",
    )(*buffers, *weights)


def add_kernel(count, *refs):
    parts, arrived, outs = refs[:count], refs[count : 2 * count], refs[2 * count :]
    for n, (part, more, out) in enumerate(zip(parts, arrived, outs)):
        cut = more.shape[0]
        at = slice(0, cut) if n % 2 == 0 else slice(cut, 2 * cut)
        rest = slice(cut, 2 * cut) if n % 2 == 0 else slice(0, cut)
        out[at, :] = (part[at, :].astype(F32) + more[...].astype(F32)).astype(BF16)
        out[rest, :] = part[rest, :]


def add_halves(parts, arrived):
    count = len(parts)
    return pl.pallas_call(
        functools.partial(add_kernel, count),
        out_shape=[jax.ShapeDtypeStruct(part.shape, BF16) for part in parts],
        in_specs=[VMEM] * (2 * count),
        out_specs=[VMEM] * count,
        compiler_params=params(VMEM_MIB),
        cost_estimate=cost(count * parts[0].size, 6 * count * parts[0].size),
        name="add_halves",
    )(*parts, *arrived)


def own_kernel(group, *refs):
    groups = len(refs) // (group + len(NEAR))
    ins, outs = refs[: groups * group], refs[groups * group :]
    for n in range(groups):
        total = ins[n * group][...].astype(F32)
        for ref in ins[n * group + 1 : (n + 1) * group]:
            total = total + ref[...].astype(F32)
        total = total.astype(BF16)
        for piece in range(len(NEAR)):
            outs[n * len(NEAR) + piece][...] = total[piece * HALF : (piece + 1) * HALF]


def add_own(groups):
    group = len(groups[0])
    width = groups[0][0].shape[1]
    count = len(groups) * len(NEAR)
    outs = pl.pallas_call(
        functools.partial(own_kernel, group),
        out_shape=[jax.ShapeDtypeStruct((HALF, width), BF16)] * count,
        in_specs=[VMEM] * (group * len(groups)),
        out_specs=[VMEM] * count,
        compiler_params=params(SMALL_MIB),
        cost_estimate=cost(count * HALF * width * group, 2 * count * HALF * width * group),
        name="add_own",
    )(*[ref for refs in groups for ref in refs])
    return [list(outs[n * len(NEAR) : (n + 1) * len(NEAR)]) for n in range(len(groups))]


def last_kernel(group, *refs):
    out_ref = refs[-1]
    for n in range(2):
        ins = refs[n * group : (n + 1) * group]
        total = ins[0][...].astype(F32)
        for ref in ins[1:]:
            total = total + ref[...].astype(F32)
        total = total.astype(BF16)
        for expert in range(HALF // 2):
            out_ref[n * HALF // 2 + expert] = total[2 * expert : 2 * expert + 2]


def add_last(first, second):
    width = first[0].shape[1]
    return pl.pallas_call(
        functools.partial(last_kernel, len(first)),
        out_shape=jax.ShapeDtypeStruct((HALF, 2, width), BF16),
        in_specs=[VMEM] * (2 * len(first)),
        out_specs=VMEM,
        compiler_params=params(SMALL_MIB),
        cost_estimate=cost(8 * HALF * width, 20 * HALF * width),
        name="add_last",
    )(*first, *second)


def along_x(step):
    return [(SIDE * y + x, SIDE * y + (x + step) % SIDE) for y in range(SIDE) for x in range(SIDE)]


def along_y(step):
    return [(SIDE * y + x, SIDE * ((y + step) % SIDE) + x) for y in range(SIDE) for x in range(SIDE)]


def send(array, pairs):
    return lax.ppermute(array, "ctx", pairs)


SMEM = pl.BlockSpec(memory_space=pltpu.SMEM)
VMEM = pl.BlockSpec(memory_space=pltpu.VMEM)


def params(mib):
    return pltpu.CompilerParams(vmem_limit_bytes=mib << 20)


def cost(flops, moved):
    return pl.CostEstimate(flops=int(flops), bytes_accessed=int(moved), transcendentals=0)


def per_device(
    queries, keys, values, out_grad, log_decay, doc_lengths, moe_input, moe_grad,
    routes, gate_weights, w_gate, w_up, w_down,
):
    length, width_all = queries.shape[1:]
    heads = log_decay.shape[1]
    size = width_all // heads
    blocks = lax.axis_size("ctx")
    experts = lax.axis_size("exp")
    tokens, width = moe_input.shape
    slots = 2 * experts
    place = lax.axis_index("ctx").astype(jnp.int32).reshape(1)
    q, k, v, g = queries[0], keys[0], values[0], out_grad[0]
    logs = log_decay[0]

    filled = pl.pallas_call(
        fill_kernel,
        out_shape=jax.ShapeDtypeStruct((experts, 2, 2 * width), BF16),
        in_specs=[SMEM, SMEM, VMEM, VMEM],
        out_specs=VMEM,
        compiler_params=params(VMEM_MIB),
        cost_estimate=cost(4 * slots * tokens * width, 8 * slots * width),
        name="fill",
    )(routes.T, gate_weights.T, moe_input, moe_grad)
    arrived = lax.all_to_all(
        filled, "exp", split_axis=0, concat_axis=0, tiled=True
    ).reshape(slots, 2 * width)

    logs, filled = lax.optimization_barrier((logs, filled))
    steps = heads // HEADS_STEP
    cols = HEADS_STEP * size
    pairs = HEADS_STEP // 2
    position_spec = pl.BlockSpec((length, cols), lambda i: (0, i))
    log_spec = pl.BlockSpec((HEADS_STEP, length), lambda i: (i, 0))
    sent_rows = 4 * size + DECAY_ROWS
    local = pl.pallas_call(
        local_kernel,
        grid=(steps,),
        out_shape=jax.ShapeDtypeStruct((heads // 2, sent_rows, size), BF16),
        in_specs=[SMEM, SMEM, log_spec] + [position_spec] * 4,
        out_specs=pl.BlockSpec((pairs, sent_rows, size), lambda i: (i, 0, 0)),
        compiler_params=params(VMEM_MIB),
        cost_estimate=cost(4 * heads * length * size * size, 12 * length * width_all),
        name="local_sums",
    )(doc_lengths, place, logs, q, k, v, g)
    arrived, _ = lax.optimization_barrier((arrived, local))

    first, second = arrived[:HALF], arrived[HALF:]
    first_near = [first] + [send(first, along_x(-d)) for d in NEAR[1:]]
    second_near = [second] + [send(second, along_y(-d)) for d in NEAR[1:]]
    first_row = [jnp.concatenate(first_near[:2]), jnp.concatenate(first_near[2:])]
    second_col = [jnp.concatenate(second_near[:2]), jnp.concatenate(second_near[2:])]
    weights = (w_gate[0], w_up[0], w_down[0])
    ways = [along_y(1), along_y(-1), along_x(1), along_x(-1)]
    both = [first_row, first_row, second_col, second_col]
    early = [send(pair[n % 2], ways[n]) for n, pair in enumerate(both)]
    far = [send(part, way) for part, way in zip(early, ways)]
    late = [send(pair[1 - n % 2], ways[n]) for n, pair in enumerate(both)]
    held = lax.optimization_barrier((*late, *far, local))
    late, far, local = list(held[:4]), list(held[4:8]), held[8]
    near = [
        early[0], late[0], late[1], early[1],
        early[2], late[2], late[3], early[3],
    ]
    *near_terms, first_own, second_own = expert_rows(near + first_row + second_col, weights, 6)
    own_heads = lax.all_to_all(local, "ctx", split_axis=0, concat_axis=0, tiled=True)
    state_spec = pl.BlockSpec((blocks, size, size), lambda i: (0, i, 0))
    scanned = pl.pallas_call(
        scan_kernel,
        grid=(4,),
        out_shape=jax.ShapeDtypeStruct((blocks, 4 * size, size), BF16),
        in_specs=[
            pl.BlockSpec((blocks, DECAY_ROWS, size), lambda i: (0, 4 * size // DECAY_ROWS, 0)),
            state_spec,
        ],
        out_specs=state_spec,
        compiler_params=params(SMALL_MIB),
        cost_estimate=cost(blocks * 8 * size * size, 16 * blocks * size * size),
        name="scan",
    )(own_heads, own_heads)

    far_terms = expert_rows(far, weights)
    arrived_far = [send(part, way) for part, way in zip(far_terms, ways)]
    up, down, left, right = near_terms
    halves = add_halves([down, up, right, left], arrived_far)
    arrived_near = [send(part, way) for part, way in zip(halves, ways)]
    *arrived_near, scanned = lax.optimization_barrier((*arrived_near, scanned))
    states = lax.all_to_all(scanned, "ctx", split_axis=0, concat_axis=0, tiled=True)
    first_sum, second_sum = add_own(
        [[first_own] + arrived_near[:2], [second_own] + arrived_near[2:]]
    )
    first_sum[0], states = lax.optimization_barrier((first_sum[0], states))
    summed = add_last(
        first_sum[:1] + [send(part, along_x(d)) for part, d in zip(first_sum[1:], NEAR[1:])],
        second_sum[:1] + [send(part, along_y(d)) for part, d in zip(second_sum[1:], NEAR[1:])],
    )
    returned = lax.all_to_all(
        summed, "exp", split_axis=0, concat_axis=0, tiled=True
    ).reshape(slots, width)
    d_moe = pl.pallas_call(
        combine_kernel,
        out_shape=jax.ShapeDtypeStruct((tokens, width), BF16),
        in_specs=[SMEM, VMEM],
        out_specs=VMEM,
        compiler_params=params(SMALL_MIB),
        cost_estimate=cost(2 * slots * tokens * width, 4 * slots * width),
        name="combine",
    )(routes.T, returned)

    grad_q, grad_k, grad_v = pl.pallas_call(
        grads_kernel,
        grid=(steps,),
        out_shape=[jax.ShapeDtypeStruct((length, width_all), BF16)] * 3,
        in_specs=[SMEM, SMEM, log_spec]
        + [position_spec] * 4
        + [pl.BlockSpec((pairs, 4 * size, size), lambda i: (i, 0, 0))],
        out_specs=[position_spec] * 3,
        compiler_params=params(VMEM_MIB),
        cost_estimate=cost(16 * heads * length * size * size, 18 * length * width_all),
        name="attention_grads",
    )(doc_lengths, place, logs, q, k, v, g, states)
    return (grad_q[None], grad_k[None], grad_v[None], d_moe)


def solution(mesh):
    rows = P("exp", "ctx", None)
    tokens = P(("ctx", "exp"), None)
    return jax.shard_map(
        per_device,
        mesh=mesh,
        in_specs=(rows, rows, rows, rows, P("exp", None, "ctx"), P("exp", None))
        + (tokens,) * 4
        + (rows,) * 3,
        out_specs=(rows, rows, rows, tokens),
        check_vma=False,
    )
```
